512 devices in a mesh: img: 128 (over x, z, core), tok: 4 (over y).
Axes of the slice: x: 4, y: 4, z: 16, core: 2. Of those that a mesh axis runs over, the one named last changes fastest.
Arguments:
- tokens: bfloat16 [128, 32, 4, 8, 1024], P('img', None, 'tok'), may hold values from -6 to 6
- pair_list: int32 [128, 2], replicated, may hold values from 0 to 127, as said below
- owner_base: int32 [128], replicated, may hold values from 0 to 127, as said below
- embed_weight: bfloat16 [1024, 768], P('img'), may hold values from -0.1875 to 0.1875
- self_project: bfloat16 [768, 1152], P('img'), may hold values from -0.375 to 0.375
- self_output: bfloat16 [384, 768], P('img'), may hold values from -0.3125 to 0.3125
- cross_query: bfloat16 [768, 384], P('img'), may hold values from -0.375 to 0.375
- cross_keyval: bfloat16 [768, 768], P('img'), may hold values from -0.375 to 0.375
- cross_output: bfloat16 [384, 768], P('img'), may hold values from -0.3125 to 0.3125
Outputs:
- features: bfloat16 [128, 32, 4, 8, 768], P('img', None, 'tok')
The draws below stay inside these ranges and needn't reach their ends.
Inputs may be any that keep to these rules, and one draw needn't show every extreme that they name: owner_base is a permutation: block g of image i is held by img index (owner_base[i] + g) mod 128. `pair_list`: every image is the first image of exactly one row; the owner_base values of a row's two images differ by 32 to 128 - 32 modulo 128.
All inputs are finite; a program needn't handle non-finite values.
Results may differ from the reference program's by a relative error of at most 0.027.
Values may be sent and summed in bfloat16 or wider, within the bound.
No kernel may reach another device: no remote copies, remote signals or barrier semaphores. Data moves between devices by JAX's collectives and lax.ppermute only.
A program may use at most 64 MiB of HBM per device.

```python
import math
import jax
import jax.numpy as jnp
from jax import lax

D = 768
E = 1024
HEADS = 6
HD = 64
TOK_IMG = 1024
SPREAD = 32
BLOCK = 8
IMAGES = 128
N_IMG = 128
N_TOK = 4


def holder_order(key):
    return jax.random.permutation(key, N_IMG).astype(jnp.int32)


def draw_owner_base(key, part):
    bases = holder_order(key)
    return bases


def draw_pair_list(key, part):
    bases = holder_order(key)
    key = jax.random.fold_in(key, 23)
    first_key, offset_key = jax.random.split(key)
    first = jax.random.permutation(first_key, N_IMG).astype(jnp.int32)
    offsets = jax.random.randint(offset_key, (N_IMG,), SPREAD, N_IMG - SPREAD + 1).astype(jnp.int32)
    inverse = jnp.argsort(bases).astype(jnp.int32)
    second = inverse[(bases[first] + offsets) % N_IMG]
    return jnp.stack([first, second], axis=1).astype(jnp.int32)


def block_scale(stream_key, extent, shards, smallest, largest):
    gain = 1.0
    for axis_at, parts in shards:
        heights = jax.random.uniform(jax.random.fold_in(jax.random.fold_in(stream_key, 6), axis_at), (parts,), jnp.float32, smallest / len(shards), largest / len(shards))
        gain = gain * jnp.repeat(jnp.exp(heights), extent[axis_at] // parts).reshape((-1,) + (1,) * (len(extent) - 1 - axis_at))
    return gain


def scatter_about(stream_key, shape, spread, reach, cuts=(), kind=jnp.bfloat16):
    drawn = jax.random.normal(stream_key, shape, jnp.float32) * spread
    if len(cuts) > 0:
        drawn = block_scale(stream_key, shape, cuts, -0.22, 0.18) * drawn
    return jnp.clip(drawn, min=-reach, max=reach).astype(kind)


def setup_inputs(seed: int = 0) -> dict:
    key_of = jax.random.split(jax.random.key(seed), 10)
    tokens = scatter_about(key_of[0], (N_IMG, SPREAD, N_TOK, BLOCK, E), 1.0, 6.0, ((0, 128), (2, 4)))
    pair_list = draw_pair_list(jax.random.fold_in(key_of[9], 71), 0)
    owner_base = draw_owner_base(jax.random.fold_in(key_of[9], 71), 0)
    embed_weight = scatter_about(key_of[3], (E, D), E ** -0.5, 0.1875, ((0, 128),))
    self_project = scatter_about(key_of[4], (D, 3 * HEADS * HD), (1.7 * D ** -0.5), 0.375, ((0, 128),))
    self_output = scatter_about(key_of[5], (HEADS * HD, D), (HEADS * HD) ** -0.5, 0.3125, ((0, 128),))
    cross_query = scatter_about(key_of[6], (D, HEADS * HD), (1.7 * D ** -0.5), 0.375, ((0, 128),))
    cross_keyval = scatter_about(key_of[7], (D, 2 * HEADS * HD), (1.7 * D ** -0.5), 0.375, ((0, 128),))
    cross_output = scatter_about(key_of[8], (HEADS * HD, D), (HEADS * HD) ** -0.5, 0.3125, ((0, 128),))
    return {"tokens": tokens, "pair_list": pair_list, "owner_base": owner_base, "embed_weight": embed_weight, "self_project": self_project, "self_output": self_output, "cross_query": cross_query, "cross_keyval": cross_keyval, "cross_output": cross_output}


def normalize(values):
    mean_value = lax.optimization_barrier(jnp.mean(values, axis=-1, keepdims=True))
    centred = values - mean_value
    variance = lax.optimization_barrier(jnp.mean(centred * centred, axis=-1, keepdims=True))
    return centred * lax.rsqrt(variance + 1e-06)

def attend(queries, keys_in, values_in):
    length = queries.shape[0]
    others = keys_in.shape[0]
    query_heads = queries.astype(jnp.float32).reshape(length, HEADS, HD)
    key_heads = keys_in.astype(jnp.float32).reshape(others, HEADS, HD)
    value_heads = values_in.astype(jnp.float32).reshape(others, HEADS, HD)
    scores = jnp.einsum('rhd,khd->hrk', query_heads, key_heads) / math.sqrt(HD)
    weights = jnp.exp(scores)
    rounded = lax.optimization_barrier(weights.astype(jnp.bfloat16)).astype(jnp.float32)
    numer = jnp.einsum('hrk,khd->rhd', rounded, value_heads)
    denom = lax.optimization_barrier(jnp.sum(weights, axis=-1))
    return (numer / jnp.transpose(denom)[:, :, None]).astype(jnp.bfloat16).reshape(length, HEADS * HD)

def reference(tokens, pair_list, owner_base, embed_weight, self_project, self_output, cross_query, cross_keyval, cross_output):
    width = HEADS * HD
    spread_index = jnp.arange(SPREAD, dtype=jnp.int32)
    holders = ((owner_base[:, None] + spread_index[None, :]) % N_IMG).astype(jnp.int32)
    image_tokens = tokens[holders, spread_index[None, :]].reshape(IMAGES, TOK_IMG, E)

    def per_image(image_rows):
        embedded = jnp.dot(image_rows, embed_weight, preferred_element_type=jnp.float32).astype(jnp.bfloat16)
        normed = normalize(embedded.astype(jnp.float32)).astype(jnp.bfloat16)
        projected = jnp.dot(normed, self_project, preferred_element_type=jnp.float32).astype(jnp.bfloat16)
        attended = attend(projected[:, :width], projected[:, width:2 * width], projected[:, 2 * width:])
        after_self = embedded.astype(jnp.float32) + jnp.dot(attended, self_output, preferred_element_type=jnp.float32)
        keyval = jnp.dot(normed, cross_keyval, preferred_element_type=jnp.float32).astype(jnp.bfloat16)
        second_normed = normalize(after_self).astype(jnp.bfloat16)
        query_rows = jnp.dot(second_normed, cross_query, preferred_element_type=jnp.float32).astype(jnp.bfloat16)
        return (after_self, query_rows, keyval)
    after_self, query_rows, keyval = lax.map(per_image, image_tokens)

    def cross(first, second):
        attended = attend(query_rows[first], keyval[second, :, :width], keyval[second, :, width:])
        mixed = after_self[first] + jnp.dot(attended, cross_output, preferred_element_type=jnp.float32)
        return mixed.astype(jnp.bfloat16)

    def add_pair(total, pair_row):
        first = pair_row[0]
        second = pair_row[1]
        total = total.at[first].add(cross(first, second).astype(jnp.float32))
        total = total.at[second].add(cross(second, first).astype(jnp.float32))
        return (total, jnp.int32(0))
    total, unused = lax.scan(add_pair, jnp.zeros((IMAGES, TOK_IMG, D), jnp.float32), pair_list)
    blocks = total.astype(jnp.bfloat16).reshape(IMAGES, SPREAD, N_TOK, BLOCK, D)
    result = jnp.zeros((N_IMG, SPREAD, N_TOK, BLOCK, D), jnp.bfloat16)
    return result.at[holders, spread_index[None, :]].set(blocks)
```

```python
import math

import jax
import jax.numpy as jnp
import numpy as np
from jax import lax
from jax.sharding import Mesh, PartitionSpec as P

HEADS = 6
HD = 64
LANES = 128
IMG = ("x", "z", "c")

SECTIONS = (
    ("embed", 8, 6),
    ("project", 6, 9),
    ("self_out", 3, 6),
    ("query", 6, 3),
    ("keyval", 6, 6),
    ("cross_out", 3, 6),
)
PACKED = sum(rows * tiles for _, rows, tiles in SECTIONS)


def normalize(values):
    mean_value = jnp.mean(values, axis=-1, keepdims=True)
    centred = values - mean_value
    variance = jnp.mean(centred * centred, axis=-1, keepdims=True)
    return centred * lax.rsqrt(variance + 1e-06)


def row_orders(toks, z_low, cores):
    quarter = PACKED // toks
    tiles = []
    at = 0
    for _, rows, count in SECTIONS:
        for _ in range(count):
            tiles.append((at, rows))
            at += rows
    orders = np.zeros((toks, quarter * z_low * cores), np.int32)
    places = []
    for tok in range(toks):
        out = 0
        for start, rows in tiles:
            if start // quarter != tok:
                continue
            assert (start + rows - 1) // quarter == tok
            places.append((tok, out, rows * z_low * cores))
            for z in range(z_low):
                for core in range(cores):
                    for row in range(rows):
                        orders[tok, out] = (core * z_low + z) * quarter + start - tok * quarter + row
                        out += 1
    return orders, places


def pack(shards_in):
    pieces = []
    for shard in shards_in:
        rows, width = shard.shape
        pieces.append(
            jnp.transpose(shard.reshape(rows, width // LANES, LANES), (1, 0, 2)).reshape(-1, LANES)
        )
    return jnp.concatenate(pieces, axis=0)


def spread_to(value, axis):
    count = lax.axis_size(axis)
    return lax.all_to_all(
        jnp.broadcast_to(value[None], (count,) + value.shape), axis, 0, 0, tiled=True
    )


def gather_weights(shards_in):
    toks, cores, depth = lax.axis_size("tok"), lax.axis_size("c"), lax.axis_size("z")
    tok = lax.axis_index("tok")
    quarter = PACKED // toks
    z_low = depth // cores
    orders, places = row_orders(toks, z_low, cores)
    mine = lax.dynamic_slice_in_dim(pack(shards_in), tok * quarter, quarter, axis=0)
    along_z = spread_to(mine, "z")
    halves = lax.all_to_all(
        along_z.reshape(cores, z_low, quarter, LANES), "c", 0, 0, tiled=True
    )
    order = lax.dynamic_index_in_dim(jnp.asarray(orders), tok, axis=0, keepdims=False)
    count = orders.shape[1]
    mover = (order[:, None] == jnp.arange(count, dtype=jnp.int32)[None, :]).astype(jnp.bfloat16)
    ordered = jnp.dot(
        mover, halves.reshape(count, LANES), preferred_element_type=jnp.float32
    ).astype(jnp.bfloat16)
    along_x = spread_to(ordered, "x")
    along_y = spread_to(along_x, "tok")
    everything = spread_to(along_y, "c")
    full = []
    next_tile = 0
    for _, _, tiles in SECTIONS:
        columns = []
        for place_tok, start, rows in places[next_tile : next_tile + tiles]:
            part = everything[:, place_tok, :, start : start + rows, :]
            columns.append(jnp.transpose(part, (1, 0, 2, 3)).reshape(-1, LANES))
        full.append(jnp.concatenate(columns, axis=1))
        next_tile += tiles
    return full


def round_ring(own):
    count = lax.axis_size("tok")
    right = [(i, (i + 1) % count) for i in range(count)]
    left = [(i, (i - 1) % count) for i in range(count)]
    half = own.shape[1] // 2
    from_left = lax.ppermute(own, "tok", right)
    from_right = lax.ppermute(own, "tok", left)
    far_low = lax.ppermute(from_left[:, :half], "tok", right)
    far_high = lax.ppermute(from_right[:, half:], "tok", left)
    return [own, from_left, from_right, far_low, far_high]


def attend(queries, keys_in, values_in):
    branches, length = queries.shape[:2]
    others = keys_in.shape[1]
    query_heads = queries.reshape(branches, length, HEADS, HD)
    key_heads = keys_in.reshape(branches, others, HEADS, HD)
    value_heads = values_in.reshape(branches, others, HEADS, HD)
    scores = jnp.einsum(
        "brhd,bkhd->bhrk", query_heads, key_heads, preferred_element_type=jnp.float32
    ) / math.sqrt(HD)
    weights = jnp.exp(scores)
    numer = jnp.einsum(
        "bhrk,bkhd->brhd",
        weights.astype(jnp.bfloat16),
        value_heads,
        preferred_element_type=jnp.float32,
    )
    denom = jnp.sum(weights, axis=-1)
    return (
        (numer / jnp.transpose(denom, (0, 2, 1))[..., None])
        .astype(jnp.bfloat16)
        .reshape(branches, length, HEADS * HD)
    )


def multiply(rows, matrix):
    return jnp.einsum("brd,de->bre", rows, matrix, preferred_element_type=jnp.float32)


def shards(tokens, pair_list, owner_base, *weight_shards):
    groups = lax.axis_size("x")
    row_devices = lax.axis_size("z") * lax.axis_size("c")
    devices = groups * row_devices
    column = lax.axis_index("z") * lax.axis_size("c") + lax.axis_index("c")
    spread, block_rows, encoder = tokens.shape[1], tokens.shape[3], tokens.shape[4]
    held = tokens.reshape(spread, block_rows, encoder)
    part = encoder // groups

    parted = jnp.transpose(held.reshape(spread, block_rows, groups, part), (2, 0, 1, 3))
    pieces = lax.all_to_all(parted, "x", 0, 0, tiled=True).reshape(devices, block_rows, part)
    full = gather_weights(weight_shards)
    embed_full, project_full, self_out_full, query_full, keyval_full, cross_out_full = full
    width, model_width = self_out_full.shape

    bases = owner_base[pair_list]
    slot = (column - bases) % spread
    source = ((bases + slot - column) // row_devices) % groups
    place = source * spread + slot
    outgoing = jnp.take(pieces, place.reshape(-1), axis=0).reshape(
        devices, 2, block_rows, part
    )
    arrived = lax.all_to_all(outgoing, IMG, 0, 0, tiled=True)
    arrived = arrived.reshape(groups, row_devices, 2, block_rows, part)
    rows_in = jnp.transpose(arrived, (2, 1, 3, 0, 4)).reshape(2, row_devices * block_rows, encoder)
    embedded = multiply(rows_in, embed_full).astype(jnp.bfloat16)
    all_embedded = jnp.concatenate(round_ring(embedded), axis=1)
    all_normed = normalize(all_embedded.astype(jnp.float32)).astype(jnp.bfloat16)
    length = embedded.shape[1]
    normed = all_normed[:, :length]
    queries = multiply(normed, project_full[:, :width]).astype(jnp.bfloat16)
    keys = multiply(all_normed, project_full[:, width : 2 * width]).astype(jnp.bfloat16)
    values = multiply(all_normed, project_full[:, 2 * width :]).astype(jnp.bfloat16)
    cross_keys = multiply(all_normed, keyval_full[:, :width]).astype(jnp.bfloat16)
    cross_values = multiply(all_normed, keyval_full[:, width:]).astype(jnp.bfloat16)
    attended = attend(queries, keys, values)
    after_self = embedded.astype(jnp.float32) + multiply(attended, self_out_full)
    second_normed = normalize(after_self).astype(jnp.bfloat16)
    cross_queries = multiply(second_normed, query_full).astype(jnp.bfloat16)
    cross_attended = attend(cross_queries[::-1], cross_keys, cross_values)[::-1]
    mixed = after_self + multiply(cross_attended, cross_out_full)

    halves = groups // 2
    result = mixed.astype(jnp.bfloat16).reshape(
        2, row_devices, block_rows, halves, model_width // halves
    )
    backward = jnp.transpose(result, (0, 3, 1, 2, 4)).reshape(
        devices, block_rows, model_width // halves
    )
    returned = lax.all_to_all(backward, IMG, 0, 0, tiled=True)
    my_half = lax.axis_index("x") // halves
    my_bases = lax.dynamic_index_in_dim(bases, my_half, axis=1, keepdims=False)
    my_slot = (column - my_bases) % spread
    my_place = ((my_bases + my_slot - column) // row_devices) % groups * spread + my_slot
    selector = (
        my_place[None, :] == jnp.arange(devices, dtype=jnp.int32)[:, None]
    ).astype(jnp.bfloat16)
    partial = jnp.einsum(
        "ge,ebd->gbd", selector, returned, preferred_element_type=jnp.float32
    ).astype(jnp.bfloat16)
    home = lax.all_to_all(
        partial.reshape(groups, spread, block_rows, model_width // halves), "x", 0, 0, tiled=True
    )
    home = home.reshape(2, halves, spread, block_rows, model_width // halves)
    total = home[0].astype(jnp.float32) + home[1].astype(jnp.float32)
    summed = jnp.transpose(total.astype(jnp.bfloat16), (1, 2, 0, 3))
    return summed.reshape(1, spread, 1, block_rows, model_width)


def solution(mesh):
    chips = Mesh(mesh.devices.reshape(4, 16, 2, 4), ("x", "z", "c", "tok"))
    rows = P(IMG, None)
    tokens = P(IMG, None, "tok", None, None)
    return jax.shard_map(
        shards,
        mesh=chips,
        in_specs=(tokens, P(), P()) + (rows,) * 6,
        out_specs=tokens,
        check_vma=False,
    )
```

```python
import functools

import jax
import jax.numpy as jnp
import numpy as np
from jax import lax
from jax.experimental import pallas as pl
from jax.experimental.pallas import tpu as pltpu
from jax.sharding import Mesh, PartitionSpec as P

HEADS = 6
HD = 64
LANES = 128
IMG = ("x", "z", "c")
VMEM_BYTES = 50 * 1024 * 1024

SECTIONS = (
    ("embed", 8, 6),
    ("project", 6, 9),
    ("self_out", 3, 6),
    ("query", 6, 3),
    ("keyval", 6, 6),
    ("cross_out", 3, 6),
)
PACKED = sum(rows * tiles for _, rows, tiles in SECTIONS)


def f32_dot(left, right):
    return jnp.dot(left, right, preferred_element_type=jnp.float32)


def normalize(values):
    mean_value = jnp.mean(values, axis=-1, keepdims=True)
    centred = values - mean_value
    variance = jnp.mean(centred * centred, axis=-1, keepdims=True)
    return centred * lax.rsqrt(variance + 1e-06)


def row_tables(toks, z_low, cores):
    quarter = PACKED // toks
    tiles = []
    at = 0
    for _, rows, count in SECTIONS:
        for _ in range(count):
            tiles.append((at, rows))
            at += rows
    table = np.zeros((3, toks, quarter * z_low * cores), np.int32)
    places = []
    for tok in range(toks):
        out = 0
        for start, rows in tiles:
            if start // quarter != tok:
                continue
            assert (start + rows - 1) // quarter == tok
            places.append((tok, out, rows * z_low * cores))
            for z in range(z_low):
                for core in range(cores):
                    for row in range(rows):
                        table[:, tok, out] = (start - tok * quarter + row, z, core)
                        out += 1
    return table, places


def pack(shards_in):
    pieces = []
    for shard in shards_in:
        rows, width = shard.shape
        pieces.append(
            jnp.transpose(shard.reshape(rows, width // LANES, LANES), (1, 0, 2)).reshape(-1, LANES)
        )
    return jnp.concatenate(pieces, axis=0)


def shifted(value, axis, pairs):
    return lax.ppermute(value, axis, pairs)


def cycle(count, shift):
    return [(i, (i + shift) % count) for i in range(count)]


def gather_weights(shards_in):
    toks, cores, depth = lax.axis_size("tok"), lax.axis_size("c"), lax.axis_size("z")
    groups = lax.axis_size("x")
    tok, core, z = lax.axis_index("tok"), lax.axis_index("c"), lax.axis_index("z")
    quarter = PACKED // toks
    z_low = depth // cores
    step = 4
    table, places = row_tables(toks, z_low, cores)
    mine = lax.dynamic_slice_in_dim(pack(shards_in), tok * quarter, quarter, axis=0)

    far = [mine] + [
        lax.ppermute(mine, "z", cycle(depth, step * s)) for s in range(1, depth // step)
    ]
    far = jnp.stack(far)
    near = [far] + [
        lax.ppermute(
            far, "z", [(i, i // step * step + (i + t) % step) for i in range(depth)]
        )
        for t in range(1, step)
    ]
    near = jnp.stack(near)
    both = jnp.stack([near, lax.ppermute(near, "c", cycle(cores, 1))])

    rows, low, from_core = lax.dynamic_index_in_dim(jnp.asarray(table), tok, axis=1, keepdims=False)
    from_z = core * z_low + low
    high_step = (z // step - from_z // step) % (depth // step)
    low_step = (z - from_z) % step
    order = (((from_core - core) % cores * step + low_step) * (depth // step) + high_step) * quarter + rows
    count = cores * depth * quarter
    mover = (order[:, None] == jnp.arange(count, dtype=jnp.int32)[None, :]).astype(jnp.bfloat16)
    ordered = f32_dot(mover, both.reshape(count, LANES)).astype(jnp.bfloat16)

    along_x = jnp.stack(
        [ordered] + [lax.ppermute(ordered, "x", cycle(groups, s)) for s in range(1, groups)]
    )
    own, left, right, far_low, far_high = round_ring(along_x, 0)
    along_y = jnp.stack([own, left, jnp.concatenate([far_low, far_high], axis=0), right])
    return along_y, lax.ppermute(along_y, "c", cycle(cores, 1)), places


def round_ring(own, axis):
    count = lax.axis_size("tok")
    half = own.shape[axis] // 2
    from_left = lax.ppermute(own, "tok", cycle(count, 1))
    from_right = lax.ppermute(own, "tok", cycle(count, -1))
    low = lax.slice_in_dim(from_left, 0, half, axis=axis)
    high = lax.slice_in_dim(from_right, half, 2 * half, axis=axis)
    far_low = lax.ppermute(low, "tok", cycle(count, 1))
    far_high = lax.ppermute(high, "tok", cycle(count, -1))
    return own, from_left, from_right, far_low, far_high


def assemble_kernel(places, at_ref, mine_ref, other_ref, *rest):
    outs, sems = rest[:-1], rest[-1]
    tok, x, core = at_ref[0], at_ref[1], at_ref[2]
    toks, groups = mine_ref.shape[0], mine_ref.shape[1]
    next_tile = 0
    for section, (_, _, tiles) in enumerate(SECTIONS):
        out = outs[section]
        for tile, (place_tok, start, rows) in enumerate(places[next_tile : next_tile + tiles]):
            tok_step = lax.rem(tok - place_tok + toks, toks)
            for x_step in range(groups):
                from_x = lax.rem(x - x_step + groups, groups)
                for source, half in ((mine_ref, core), (other_ref, 1 - core)):
                    pltpu.make_async_copy(
                        source.at[tok_step, x_step, pl.ds(start, rows)],
                        out.at[from_x, half, :, pl.ds(tile * LANES, LANES)],
                        sems.at[section],
                    ).start()
        next_tile += tiles
    for section in range(len(SECTIONS)):
        pltpu.make_async_copy(outs[section], outs[section], sems.at[section]).wait()


def assemble(mine, other, places):
    groups = mine.shape[1]
    cores = lax.axis_size("c")
    place = jnp.stack(
        [lax.axis_index("tok"), lax.axis_index("x"), lax.axis_index("c")]
    ).astype(jnp.int32)
    shapes = []
    next_tile = 0
    for _, _, tiles in SECTIONS:
        rows = places[next_tile][2]
        shapes.append(jax.ShapeDtypeStruct((groups, cores, rows, tiles * LANES), jnp.bfloat16))
        next_tile += tiles
    full = pl.pallas_call(
        functools.partial(assemble_kernel, places),
        out_shape=shapes,
        in_specs=[pl.BlockSpec(memory_space=pltpu.SMEM)] + [pl.BlockSpec(memory_space=pl.ANY)] * 2,
        out_specs=[pl.BlockSpec(memory_space=pl.ANY)] * len(shapes),
        scratch_shapes=[pltpu.SemaphoreType.DMA((len(SECTIONS),))],
        cost_estimate=pl.CostEstimate(
            flops=0, bytes_accessed=4 * mine.size * 2, transcendentals=0
        ),
        name="assemble",
    )(place, mine, other)
    return [matrix.reshape(-1, matrix.shape[-1]) for matrix in full]


def embed_kernel(arrived_ref, matrix_ref, out_ref):
    groups, blocks, images, block_rows, part = arrived_ref.shape
    for image in range(images):
        total = None
        for group in range(groups):
            rows = arrived_ref[group, :, image].astype(jnp.float32)
            rows = rows.reshape(blocks * block_rows, part).astype(jnp.bfloat16)
            product = f32_dot(rows, matrix_ref[group * part : (group + 1) * part, :])
            total = product if total is None else total + product
        out_ref[image] = total.astype(jnp.bfloat16)


def embed(arrived, matrix):
    groups, blocks, images, block_rows, part = arrived.shape
    rows, width = blocks * block_rows, matrix.shape[1]
    return pl.pallas_call(
        embed_kernel,
        out_shape=jax.ShapeDtypeStruct((images, rows, width), jnp.bfloat16),
        compiler_params=pltpu.CompilerParams(vmem_limit_bytes=VMEM_BYTES),
        cost_estimate=pl.CostEstimate(
            flops=2 * images * rows * matrix.size,
            bytes_accessed=2 * (arrived.size + matrix.size + images * rows * width),
            transcendentals=0,
        ),
        name="embed",
    )(arrived, matrix)


def attend(queries, key_ref, value_ref, first_key, first_value, chunk):
    rows = queries.shape[0]
    others = key_ref.shape[0]
    low_half = lax.broadcasted_iota(jnp.int32, (1, LANES), 1) < HD
    done = []
    for pair in range(HEADS * HD // LANES):
        query = queries[:, pair * LANES : (pair + 1) * LANES]
        blank = jnp.zeros_like(query)
        low_query = jnp.where(low_half, query, blank)
        high_query = jnp.where(low_half, blank, query)
        low_total = jnp.zeros((rows, LANES), jnp.float32)
        high_total = jnp.zeros((rows, LANES), jnp.float32)
        for start in range(0, others, chunk):
            at = slice(start, start + chunk)
            keys = key_ref[at, first_key + pair * LANES : first_key + (pair + 1) * LANES]
            values = value_ref[at, first_value + pair * LANES : first_value + (pair + 1) * LANES]
            ones = jnp.ones_like(values)
            across = (((1,), (1,)), ((), ()))
            scores = lax.dot_general(low_query, keys, across, preferred_element_type=jnp.float32)
            weights = jnp.exp(scores).astype(jnp.bfloat16)
            low_total += f32_dot(weights, jnp.where(low_half, values, ones))
            scores = lax.dot_general(high_query, keys, across, preferred_element_type=jnp.float32)
            weights = jnp.exp(scores).astype(jnp.bfloat16)
            high_total += f32_dot(weights, jnp.where(low_half, ones, values))
        numer = jnp.where(low_half, low_total, high_total)
        denom = pltpu.roll(jnp.where(low_half, high_total, low_total), HD, 1)
        done.append((numer / denom).astype(jnp.bfloat16))
    return jnp.concatenate(done, axis=1)


def scaled(queries):
    return (queries.astype(jnp.bfloat16).astype(jnp.float32) * HD**-0.5).astype(jnp.bfloat16)


def self_kernel(
    own_ref, left_ref, right_ref, low_ref, high_ref,
    project_ref, output_ref, query_ref, keyval_ref,
    after_ref, second_ref, cross_ref,
    keyval_scratch,
):
    width = output_ref.shape[0]
    own = own_ref[0].astype(jnp.float32)
    rows = own.shape[0]
    normed = normalize(own).astype(jnp.bfloat16)
    queries = scaled(f32_dot(normed, project_ref[:, :width]))
    at = 0
    for ref in (own_ref, left_ref, right_ref, low_ref, high_ref):
        if at > 0:
            normed = normalize(ref[0].astype(jnp.float32)).astype(jnp.bfloat16)
        here = slice(at, at + normed.shape[0])
        keyval_scratch[here] = f32_dot(normed, project_ref[:, width:]).astype(jnp.bfloat16)
        cross_ref[0, here] = f32_dot(normed, keyval_ref[...]).astype(jnp.bfloat16)
        at += normed.shape[0]
    attended = attend(queries, keyval_scratch, keyval_scratch, 0, width, 256)
    after = own + f32_dot(attended, output_ref[...])
    after_ref[0] = after
    second = normalize(after).astype(jnp.bfloat16)
    second_ref[0] = scaled(f32_dot(second, query_ref[...]))


def self_block(pieces, project, output, query, keyval):
    own = pieces[0]
    images, rows, model = own.shape
    width = output.shape[0]
    everyone = sum(piece.shape[1] for piece in pieces)

    def one(shape):
        return pl.BlockSpec((1,) + shape[1:], lambda i: (i, 0, 0))

    def whole(matrix):
        return pl.BlockSpec(matrix.shape, lambda i: (0, 0))

    matrices = (project, output, query, keyval)
    shapes = [
        jax.ShapeDtypeStruct((images, rows, model), jnp.float32),
        jax.ShapeDtypeStruct((images, rows, width), jnp.bfloat16),
        jax.ShapeDtypeStruct((images, everyone, 2 * width), jnp.bfloat16),
    ]
    flops = 2 * images * (
        everyone * model * 4 * width + rows * model * 3 * width + 2 * rows * everyone * width
    )
    return pl.pallas_call(
        self_kernel,
        grid=(images,),
        out_shape=shapes,
        in_specs=[one(piece.shape) for piece in pieces] + [whole(matrix) for matrix in matrices],
        out_specs=[one(shape.shape) for shape in shapes],
        scratch_shapes=[pltpu.VMEM((everyone, 2 * width), jnp.bfloat16)],
        compiler_params=pltpu.CompilerParams(vmem_limit_bytes=VMEM_BYTES),
        cost_estimate=pl.CostEstimate(
            flops=flops,
            bytes_accessed=2 * sum(matrix.size for matrix in matrices) + 8 * own.size,
            transcendentals=images * HEADS * rows * everyone,
        ),
        name="self_block",
    )(*pieces, *matrices)


def cross_kernel(after_ref, query_ref, keyval_ref, output_ref, out_ref):
    width, model = output_ref.shape
    halves, blocks, block_rows, part = out_ref.shape[1:]
    keyval = keyval_ref.at[0]
    attended = attend(query_ref[0], keyval, keyval, 0, width, 256)
    mixed = after_ref[0] + f32_dot(attended, output_ref[...])
    for half in range(halves):
        columns = mixed[:, half * part : (half + 1) * part]
        out_ref[0, half] = columns.reshape(blocks, block_rows, part).astype(jnp.bfloat16)


def cross_block(after, query, keyval, output, halves, block_rows):
    images, rows, model = after.shape
    width = output.shape[0]
    everyone = keyval.shape[1]
    shape = (images, halves, rows // block_rows, block_rows, model // halves)
    return pl.pallas_call(
        cross_kernel,
        grid=(images,),
        out_shape=jax.ShapeDtypeStruct(shape, jnp.bfloat16),
        in_specs=[
            pl.BlockSpec((1, rows, model), lambda i: (i, 0, 0)),
            pl.BlockSpec((1, rows, width), lambda i: (i, 0, 0)),
            pl.BlockSpec((1, everyone, 2 * width), lambda i: (images - 1 - i, 0, 0)),
            pl.BlockSpec(output.shape, lambda i: (0, 0)),
        ],
        out_specs=pl.BlockSpec((1,) + shape[1:], lambda i: (i, 0, 0, 0, 0)),
        compiler_params=pltpu.CompilerParams(vmem_limit_bytes=VMEM_BYTES),
        cost_estimate=pl.CostEstimate(
            flops=2 * images * (2 * rows * everyone * width + rows * model * width),
            bytes_accessed=4 * after.size + 2 * (query.size + keyval.size + output.size + after.size),
            transcendentals=images * HEADS * rows * everyone,
        ),
        name="cross_block",
    )(after, query, keyval, output)


def shards(tokens, pair_list, owner_base, *weight_shards):
    groups = lax.axis_size("x")
    row_devices = lax.axis_size("z") * lax.axis_size("c")
    devices = groups * row_devices
    column = lax.axis_index("z") * lax.axis_size("c") + lax.axis_index("c")
    spread, block_rows, encoder = tokens.shape[1], tokens.shape[3], tokens.shape[4]
    held = tokens.reshape(spread, block_rows, encoder)
    part = encoder // groups

    parted = jnp.stack([held[:, :, x * part : (x + 1) * part] for x in range(groups)])
    pieces = lax.all_to_all(parted, "x", 0, 0, tiled=True).reshape(devices, block_rows, part)

    bases = owner_base[pair_list]
    slot = (column - bases) % spread
    source = ((bases + slot - column) // row_devices) % groups
    place = source * spread + slot
    outgoing = jnp.take(pieces, place.reshape(-1), axis=0, mode="clip").reshape(
        devices, 2, block_rows, part
    )
    arrived = lax.all_to_all(outgoing, IMG, 0, 0, tiled=True)
    arrived = arrived.reshape(groups, row_devices, 2, block_rows, part)

    full = assemble(*gather_weights(weight_shards))
    embed_full, project_full, self_out_full, query_full, keyval_full, cross_out_full = full
    model_width = embed_full.shape[1]

    embedded = embed(arrived, embed_full)
    after_self, cross_queries, cross_keyval = self_block(
        round_ring(embedded, 1), project_full, self_out_full, query_full, keyval_full
    )

    halves = groups // 2
    backward = cross_block(
        after_self, cross_queries, cross_keyval, cross_out_full, halves, block_rows
    ).reshape(devices, block_rows, model_width // halves)
    returned = lax.all_to_all(backward, IMG, 0, 0, tiled=True)
    my_half = lax.axis_index("x") // halves
    my_place = lax.dynamic_index_in_dim(place, my_half, axis=1, keepdims=False)
    selector = (
        my_place[None, :] == jnp.arange(devices, dtype=jnp.int32)[:, None]
    ).astype(jnp.bfloat16)
    partial = jnp.einsum(
        "ge,ebd->gbd", selector, returned, preferred_element_type=jnp.float32
    ).astype(jnp.bfloat16)
    home = lax.all_to_all(
        partial.reshape(groups, spread, block_rows, model_width // halves), "x", 0, 0, tiled=True
    )
    home = home.reshape(2, halves, spread, block_rows, model_width // halves)
    total = home[0].astype(jnp.float32) + home[1].astype(jnp.float32)
    summed = jnp.concatenate([total[half] for half in range(halves)], axis=-1)
    return summed.astype(jnp.bfloat16).reshape(1, spread, 1, block_rows, model_width)


def solution(mesh):
    chips = Mesh(mesh.devices.reshape(4, 16, 2, 4), ("x", "z", "c", "tok"))
    rows = P(IMG, None)
    tokens = P(IMG, None, "tok", None, None)
    return jax.shard_map(
        shards,
        mesh=chips,
        in_specs=(tokens, P(), P()) + (rows,) * 6,
        out_specs=tokens,
        check_vma=False,
    )
```

```python
import functools

import jax
import jax.numpy as jnp
import numpy as np
from jax import lax
from jax.experimental import pallas as pl
from jax.experimental.pallas import tpu as pltpu
from jax.sharding import Mesh, PartitionSpec as P

HEADS = 6
HD = 64
LANES = 128
IMG = ("x", "z", "c")
VMEM_BYTES = 50 * 1024 * 1024

SECTIONS = (
    ("embed", 8, 6),
    ("project", 6, 9),
    ("self_out", 3, 6),
    ("query", 6, 3),
    ("keyval", 6, 6),
    ("cross_out", 3, 6),
)
def f32_dot(left, right):
    return jnp.dot(left, right, preferred_element_type=jnp.float32)


def normalize(values):
    mean_value = jnp.mean(values, axis=-1, keepdims=True)
    centred = values - mean_value
    variance = jnp.mean(centred * centred, axis=-1, keepdims=True)
    return centred * lax.rsqrt(variance + 1e-06)


def row_tables(sections, toks, z_low, cores):
    total = sum(rows * tiles for _, rows, tiles in sections)
    quarter = total // toks
    table = np.zeros((3, toks, quarter * z_low * cores), np.int32)
    places = []
    at = 0
    for _, rows, tiles in sections:
        places.append([])
        for _ in range(tiles):
            tok, start = divmod(at, quarter)
            assert start + rows <= quarter
            out = start * z_low * cores
            places[-1].append((tok, out, rows * z_low * cores))
            for z in range(z_low):
                for core in range(cores):
                    for row in range(rows):
                        table[:, tok, out] = (start + row, z, core)
                        out += 1
            at += rows
    return table, places, quarter


def pack_kernel(sections, toks, tok_ref, *refs):
    shard_refs, out_ref = refs[:-1], refs[-1]
    pieces = []
    for ref, (_, _, tiles) in zip(shard_refs, sections):
        for tile in range(tiles):
            pieces.append((ref, slice(tile * LANES, (tile + 1) * LANES)))
    quarter = out_ref.shape[0]

    def taken(some):
        values = [ref[:, at].astype(jnp.float32) for ref, at in some]
        return jnp.concatenate(values, axis=0).astype(jnp.bfloat16)

    groups = [[] for _ in range(toks)]
    at = 0
    for ref, columns in pieces:
        groups[at // quarter].append((ref, columns))
        at += ref.shape[0]
    for tok in range(toks):
        @pl.when(tok_ref[0] == tok)
        def _(tok=tok):
            out_ref[...] = taken(groups[tok])


def pack(shards_in, sections, toks):
    quarter = sum(rows * tiles for _, rows, tiles in sections) // toks
    tok = jnp.zeros((1,), jnp.int32) if toks == 1 else lax.axis_index("tok").astype(jnp.int32)[None]
    return pl.pallas_call(
        functools.partial(pack_kernel, sections, toks),
        out_shape=jax.ShapeDtypeStruct((quarter, LANES), jnp.bfloat16),
        in_specs=[pl.BlockSpec(memory_space=pltpu.SMEM)]
        + [pl.BlockSpec(memory_space=pltpu.VMEM)] * len(shards_in),
        out_specs=pl.BlockSpec(memory_space=pltpu.VMEM),
        name="pack",
    )(tok, *shards_in)


def cycle(count, shift):
    return [(i, (i + shift) % count) for i in range(count)]


def swap_cores(value):
    return lax.ppermute(value, "c", cycle(lax.axis_size("c"), 1))


def start_weights(shards_in):
    packed = jnp.concatenate(
        [
            pack(shards_in[:1], SECTIONS[:1], 1),
            pack(shards_in[1:], SECTIONS[1:], lax.axis_size("tok")),
        ],
        axis=0,
    )
    return lax.all_gather(packed, "z", axis=0, tiled=False)


def order_weights(along_z):
    toks, cores = lax.axis_size("tok"), lax.axis_size("c")
    tok, core = lax.axis_index("tok"), lax.axis_index("c")
    depth, packed_rows, lanes = along_z.shape
    z_low = depth // cores
    first_table, _, first_rows = row_tables(SECTIONS[:1], 1, z_low, cores)
    rest_table, _, _ = row_tables(SECTIONS[1:], toks, z_low, cores)
    rest = lax.dynamic_index_in_dim(jnp.asarray(rest_table), tok, axis=1, keepdims=False)
    rest = rest + jnp.asarray([[first_rows], [0], [0]], jnp.int32)
    rows, low, from_core = jnp.concatenate([jnp.asarray(first_table[:, 0]), rest], axis=1)
    mine = lax.dynamic_slice_in_dim(along_z, core * z_low, z_low, axis=0)
    theirs = lax.dynamic_slice_in_dim(along_z, (1 - core) * z_low, z_low, axis=0)
    both = jnp.stack([mine, swap_cores(theirs)])
    order = ((from_core - core) % cores * z_low + low) * packed_rows + rows
    count = cores * z_low * packed_rows
    mover = (order[:, None] == jnp.arange(count, dtype=jnp.int32)[None, :]).astype(jnp.bfloat16)
    ordered = f32_dot(mover, both.reshape(count, lanes)).astype(jnp.bfloat16)
    return ordered, first_table.shape[2]


def spread_weights(ordered, first_rows):
    groups = lax.axis_size("x")
    along_x = [ordered] + [lax.ppermute(ordered, "x", cycle(groups, s)) for s in range(1, groups)]
    first = jnp.stack([piece[:first_rows] for piece in along_x])
    first_full = assemble(first[None], swap_cores(first)[None], SECTIONS[:1], 1)
    rest = jnp.stack([piece[first_rows:] for piece in along_x])
    own, left, right, far_low, far_high = round_ring(rest, 0)
    along_y = jnp.stack([own, left, jnp.concatenate([far_low, far_high], axis=0), right])
    return first_full + assemble(
        along_y, swap_cores(along_y), SECTIONS[1:], lax.axis_size("tok")
    )


def round_ring(own, axis):
    count = lax.axis_size("tok")
    half = own.shape[axis] // 2
    from_left = lax.ppermute(own, "tok", cycle(count, 1))
    from_right = lax.ppermute(own, "tok", cycle(count, -1))
    low = lax.slice_in_dim(from_left, 0, half, axis=axis)
    high = lax.slice_in_dim(from_right, half, 2 * half, axis=axis)
    far_low = lax.ppermute(low, "tok", cycle(count, 1))
    far_high = lax.ppermute(high, "tok", cycle(count, -1))
    return own, from_left, from_right, far_low, far_high


def assemble_kernel(places, at_ref, mine_ref, other_ref, *outs):
    toks, groups = mine_ref.shape[:2]
    tok, x, core = at_ref[0], at_ref[1], at_ref[2]
    for out, tiles in zip(outs, places):
        for tile, (place_tok, start, rows) in enumerate(tiles):
            tok_step = lax.rem(tok - place_tok + toks, toks) if toks > 1 else 0
            for x_step in range(groups):
                from_x = lax.rem(x - x_step + groups, groups)
                for source, half in ((mine_ref, core), (other_ref, 1 - core)):
                    out[from_x, half, :, tile * LANES : (tile + 1) * LANES] = source[
                        tok_step, x_step, start : start + rows, :
                    ]


def assemble(mine, other, sections, toks):
    groups = mine.shape[1]
    cores = lax.axis_size("c")
    _, places, _ = row_tables(sections, toks, lax.axis_size("z") // cores, cores)
    place = jnp.stack(
        [lax.axis_index("tok"), lax.axis_index("x"), lax.axis_index("c")]
    ).astype(jnp.int32)
    shapes = [
        jax.ShapeDtypeStruct((groups, cores, tiles[0][2], len(tiles) * LANES), jnp.bfloat16)
        for tiles in places
    ]
    full = pl.pallas_call(
        functools.partial(assemble_kernel, places),
        out_shape=shapes,
        in_specs=[pl.BlockSpec(memory_space=pltpu.SMEM)]
        + [pl.BlockSpec(memory_space=pltpu.VMEM)] * 2,
        out_specs=[pl.BlockSpec(memory_space=pltpu.VMEM)] * len(shapes),
        compiler_params=pltpu.CompilerParams(vmem_limit_bytes=VMEM_BYTES),
        cost_estimate=pl.CostEstimate(
            flops=0, bytes_accessed=4 * mine.size * 2, transcendentals=0
        ),
        name="assemble",
    )(place, mine, other)
    return [matrix.reshape(-1, matrix.shape[-1]) for matrix in full]


def embed_kernel(arrived_ref, matrix_ref, out_ref):
    groups, blocks, images, block_rows, part = arrived_ref.shape
    for image in range(images):
        total = None
        for group in range(groups):
            rows = arrived_ref[group, :, image].astype(jnp.float32)
            rows = rows.reshape(blocks * block_rows, part).astype(jnp.bfloat16)
            product = f32_dot(rows, matrix_ref[group * part : (group + 1) * part, :])
            total = product if total is None else total + product
        out_ref[image] = total.astype(jnp.bfloat16)


def embed(arrived, matrix):
    groups, blocks, images, block_rows, part = arrived.shape
    rows, width = blocks * block_rows, matrix.shape[1]
    return pl.pallas_call(
        embed_kernel,
        out_shape=jax.ShapeDtypeStruct((images, rows, width), jnp.bfloat16),
        compiler_params=pltpu.CompilerParams(vmem_limit_bytes=VMEM_BYTES),
        cost_estimate=pl.CostEstimate(
            flops=2 * images * rows * matrix.size,
            bytes_accessed=2 * (arrived.size + matrix.size + images * rows * width),
            transcendentals=0,
        ),
        name="embed",
    )(arrived, matrix)


def head_halves():
    return lax.broadcasted_iota(jnp.int32, (1, LANES), 1) < HD


def fold(queries, key_ref, value_ref, first_key, first_value, totals, chunk=256):
    others = key_ref.shape[0]
    low_half = head_halves()
    across = (((1,), (1,)), ((), ()))
    done = []
    for pair in range(HEADS // 2):
        query = queries[:, pair * LANES : (pair + 1) * LANES]
        blank = jnp.zeros_like(query)
        low_query = jnp.where(low_half, query, blank)
        high_query = jnp.where(low_half, blank, query)
        low_total, high_total = totals[2 * pair], totals[2 * pair + 1]
        for start in range(0, others, chunk):
            at = slice(start, start + chunk)
            keys = key_ref[at, first_key + pair * LANES : first_key + (pair + 1) * LANES]
            values = value_ref[at, first_value + pair * LANES : first_value + (pair + 1) * LANES]
            ones = jnp.ones_like(values)
            scores = lax.dot_general(low_query, keys, across, preferred_element_type=jnp.float32)
            weights = jnp.exp(scores).astype(jnp.bfloat16)
            low_total = low_total + f32_dot(weights, jnp.where(low_half, values, ones))
            scores = lax.dot_general(high_query, keys, across, preferred_element_type=jnp.float32)
            weights = jnp.exp(scores).astype(jnp.bfloat16)
            high_total = high_total + f32_dot(weights, jnp.where(low_half, ones, values))
        done += [low_total, high_total]
    return done


def finish(totals):
    low_half = head_halves()
    done = []
    for pair in range(HEADS // 2):
        low_total, high_total = totals[2 * pair], totals[2 * pair + 1]
        numer = jnp.where(low_half, low_total, high_total)
        denom = pltpu.roll(jnp.where(low_half, high_total, low_total), HD, 1)
        done.append((numer / denom).astype(jnp.bfloat16))
    return jnp.concatenate(done, axis=1)


def nothing(rows):
    return [jnp.zeros((rows, LANES), jnp.float32)] * HEADS


def scaled(queries):
    return (queries.astype(jnp.bfloat16).astype(jnp.float32) * HD**-0.5).astype(jnp.bfloat16)


def self_kernel(first, last, pieces, *refs):
    refs = list(refs)
    piece_refs = [refs.pop(0) for _ in range(pieces)]
    if not first:
        query_ref, totals_in = refs.pop(0), refs.pop(0)
    if last:
        own_ref = refs.pop(0)
    project_ref, keyval_ref = refs.pop(0), refs.pop(0)
    width = keyval_ref.shape[1] // 2
    if last:
        output_ref, second_ref = refs.pop(0), refs.pop(0)
    cross_ref = refs.pop(0)
    if first:
        query_out = refs.pop(0)
    if last:
        after_ref, next_ref = refs.pop(0), refs.pop(0)
    else:
        totals_out = refs.pop(0)
    scratch = refs.pop(0)
    at = 0
    for ref in piece_refs:
        normed = normalize(ref[0].astype(jnp.float32)).astype(jnp.bfloat16)
        here = slice(at, at + normed.shape[0])
        scratch[here] = f32_dot(normed, project_ref[:, width:]).astype(jnp.bfloat16)
        cross_ref[0, here] = f32_dot(normed, keyval_ref[...]).astype(jnp.bfloat16)
        at += normed.shape[0]
    if first:
        queries = scaled(f32_dot(normed, project_ref[:, :width]))
        query_out[0] = queries
        totals = nothing(queries.shape[0])
    else:
        queries = query_ref[0]
        totals = [totals_in[0, head] for head in range(HEADS)]
    totals = fold(queries, scratch, scratch, 0, width, totals)
    if last:
        after = own_ref[0].astype(jnp.float32) + f32_dot(finish(totals), output_ref[...])
        after_ref[0] = after
        second = normalize(after).astype(jnp.bfloat16)
        next_ref[0] = scaled(f32_dot(second, second_ref[...]))
    else:
        for head in range(HEADS):
            totals_out[0, head] = totals[head]


def per_image(shape):
    return pl.BlockSpec((1,) + shape[1:], lambda i: (i,) + (0,) * (len(shape) - 1))


def whole(matrix):
    return pl.BlockSpec(matrix.shape, lambda i: (0, 0))


def self_step(pieces, project, keyval, carry=None, ending=None):
    first, last = carry is None, ending is not None
    images, _, model = pieces[0].shape
    width = keyval.shape[1] // 2
    others = sum(piece.shape[1] for piece in pieces)
    arrays = list(pieces) + list(carry or ())
    matrices = [project, keyval]
    if last:
        arrays.append(ending[0])
        matrices += ending[1:]
    rows = pieces[0].shape[1] if first else carry[0].shape[1]
    shapes = [jax.ShapeDtypeStruct((images, others, 2 * width), jnp.bfloat16)]
    if first:
        shapes.append(jax.ShapeDtypeStruct((images, rows, width), jnp.bfloat16))
    if last:
        shapes.append(jax.ShapeDtypeStruct((images, rows, model), jnp.float32))
        shapes.append(jax.ShapeDtypeStruct((images, rows, width), jnp.bfloat16))
    else:
        shapes.append(jax.ShapeDtypeStruct((images, HEADS, rows, LANES), jnp.float32))
    return pl.pallas_call(
        functools.partial(self_kernel, first, last, len(pieces)),
        grid=(images,),
        out_shape=shapes,
        in_specs=[per_image(array.shape) for array in arrays] + [whole(matrix) for matrix in matrices],
        out_specs=[per_image(shape.shape) for shape in shapes],
        scratch_shapes=[pltpu.VMEM((others, 2 * width), jnp.bfloat16)],
        compiler_params=pltpu.CompilerParams(vmem_limit_bytes=VMEM_BYTES),
        cost_estimate=pl.CostEstimate(
            flops=2 * images * (others * model * 4 * width + 4 * rows * others * width),
            bytes_accessed=2 * sum(matrix.size for matrix in matrices)
            + sum(array.size * array.dtype.itemsize for array in arrays),
            transcendentals=images * HEADS * rows * others,
        ),
        name="self_step",
    )(*arrays, *matrices)


def cross_kernel(pieces, after_ref, query_ref, *refs):
    keyval_refs, output_ref, out_ref = refs[:pieces], refs[pieces], refs[pieces + 1]
    width = output_ref.shape[0]
    halves, blocks, block_rows, part = out_ref.shape[1:]
    queries = query_ref[0]
    totals = nothing(queries.shape[0])
    for ref in keyval_refs:
        keyval = ref.at[0]
        totals = fold(queries, keyval, keyval, 0, width, totals)
    mixed = after_ref[0] + f32_dot(finish(totals), output_ref[...])
    for half in range(halves):
        columns = mixed[:, half * part : (half + 1) * part]
        out_ref[0, half] = columns.reshape(blocks, block_rows, part).astype(jnp.bfloat16)


def cross_block(after, query, keyvals, output, halves, block_rows):
    images, rows, model = after.shape
    width = output.shape[0]
    everyone = sum(keyval.shape[1] for keyval in keyvals)
    shape = (images, halves, rows // block_rows, block_rows, model // halves)
    return pl.pallas_call(
        functools.partial(cross_kernel, len(keyvals)),
        grid=(images,),
        out_shape=jax.ShapeDtypeStruct(shape, jnp.bfloat16),
        in_specs=[per_image(after.shape), per_image(query.shape)]
        + [
            pl.BlockSpec((1,) + keyval.shape[1:], lambda i: (images - 1 - i, 0, 0))
            for keyval in keyvals
        ]
        + [whole(output)],
        out_specs=per_image(shape),
        compiler_params=pltpu.CompilerParams(vmem_limit_bytes=VMEM_BYTES),
        cost_estimate=pl.CostEstimate(
            flops=2 * images * (4 * rows * everyone * width + rows * model * width),
            bytes_accessed=4 * after.size + 2 * (query.size + output.size + after.size),
            transcendentals=images * HEADS * rows * everyone,
        ),
        name="cross_block",
    )(after, query, *keyvals, output)


def shards(tokens, pair_list, owner_base, *weight_shards):
    groups = lax.axis_size("x")
    row_devices = lax.axis_size("z") * lax.axis_size("c")
    devices = groups * row_devices
    column = lax.axis_index("z") * lax.axis_size("c") + lax.axis_index("c")
    spread, block_rows, encoder = tokens.shape[1], tokens.shape[3], tokens.shape[4]
    held = tokens.reshape(spread, block_rows, encoder)
    part = encoder // groups

    parted = jnp.stack([held[:, :, x * part : (x + 1) * part] for x in range(groups)])
    parted, weight_shards = lax.optimization_barrier((parted, weight_shards))
    pieces = lax.all_to_all(parted, "x", 0, 0, tiled=True).reshape(devices, block_rows, part)
    along_z = start_weights(weight_shards)
    pieces, along_z = lax.optimization_barrier((pieces, along_z))

    bases = owner_base[pair_list]
    slot = (column - bases) % spread
    source = ((bases + slot - column) // row_devices) % groups
    place = source * spread + slot
    outgoing = jnp.take(pieces, place.reshape(-1), axis=0, mode="clip").reshape(
        devices, 2, block_rows, part
    )
    ordered, first_rows = order_weights(along_z)
    outgoing, ordered = lax.optimization_barrier((outgoing, ordered))
    arrived = lax.all_to_all(outgoing, IMG, 0, 0, tiled=True)
    arrived = arrived.reshape(groups, row_devices, 2, block_rows, part)
    full = spread_weights(ordered, first_rows)
    embed_full, project_full, self_out_full, query_full, keyval_full, cross_out_full = full
    model_width = embed_full.shape[1]

    embedded = embed(arrived, embed_full)
    own, left, right, far_low, far_high = round_ring(embedded, 1)
    near_keyval, queries, totals = self_step([own], project_full, keyval_full)
    next_keyval, totals = self_step([left, right], project_full, keyval_full, (queries, totals))
    far_keyval, after_self, cross_queries = self_step(
        [far_low, far_high], project_full, keyval_full, (queries, totals),
        (own, self_out_full, query_full),
    )

    halves = groups // 2
    backward = cross_block(
        after_self, cross_queries, [near_keyval, next_keyval, far_keyval], cross_out_full,
        halves, block_rows,
    ).reshape(devices, block_rows, model_width // halves)
    returned = lax.all_to_all(backward, IMG, 0, 0, tiled=True)
    my_half = lax.axis_index("x") // halves
    my_place = lax.dynamic_index_in_dim(place, my_half, axis=1, keepdims=False)
    selector = (
        my_place[None, :] == jnp.arange(devices, dtype=jnp.int32)[:, None]
    ).astype(jnp.bfloat16)
    partial = jnp.einsum(
        "ge,ebd->gbd", selector, returned, preferred_element_type=jnp.float32
    ).astype(jnp.bfloat16)
    home = lax.all_to_all(
        partial.reshape(groups, spread, block_rows, model_width // halves), "x", 0, 0, tiled=True
    )
    home = home.reshape(2, halves, spread, block_rows, model_width // halves)
    total = home[0].astype(jnp.float32) + home[1].astype(jnp.float32)
    summed = jnp.concatenate([total[half] for half in range(halves)], axis=-1)
    return summed.astype(jnp.bfloat16).reshape(1, spread, 1, block_rows, model_width)


def solution(mesh):
    chips = Mesh(mesh.devices.reshape(4, 16, 2, 4), ("x", "z", "c", "tok"))
    rows = P(IMG, None)
    tokens = P(IMG, None, "tok", None, None)
    return jax.shard_map(
        shards,
        mesh=chips,
        in_specs=(tokens, P(), P()) + (rows,) * 6,
        out_specs=tokens,
        check_vma=False,
    )
```

```python
import functools

import jax
import jax.numpy as jnp
import numpy as np
from jax import lax
from jax.experimental import pallas as pl
from jax.experimental.pallas import tpu as pltpu
from jax.sharding import Mesh, PartitionSpec as P

HEADS = 6
HD = 64
LANES = 128
IMG = ("x", "z", "c")
NEAR = 4
VMEM_BYTES = 50 * 1024 * 1024

SECTIONS = (
    ("embed", 8, 6),
    ("project", 6, 9),
    ("self_out", 3, 6),
    ("query", 6, 3),
    ("keyval", 6, 6),
    ("cross_out", 3, 6),
)
def f32_dot(left, right):
    return jnp.dot(left, right, preferred_element_type=jnp.float32)


def normalize(values):
    mean_value = jnp.mean(values, axis=-1, keepdims=True)
    centred = values - mean_value
    variance = jnp.mean(centred * centred, axis=-1, keepdims=True)
    return centred * lax.rsqrt(variance + 1e-06)


def row_tables(sections, toks, z_low, cores):
    total = sum(rows * tiles for _, rows, tiles in sections)
    quarter = total // toks
    table = np.zeros((3, toks, quarter * z_low * cores), np.int32)
    places = []
    at = 0
    for _, rows, tiles in sections:
        places.append([])
        for _ in range(tiles):
            tok, start = divmod(at, quarter)
            assert start + rows <= quarter
            out = start * z_low * cores
            places[-1].append((tok, out, rows * z_low * cores))
            for z in range(z_low):
                for core in range(cores):
                    for row in range(rows):
                        table[:, tok, out] = (start + row, z, core)
                        out += 1
            at += rows
    return table, places, quarter


def pack_kernel(sections, toks, tok_ref, *refs):
    shard_refs, out_ref = refs[:-1], refs[-1]
    pieces = []
    for ref, (_, _, tiles) in zip(shard_refs, sections):
        for tile in range(tiles):
            pieces.append((ref, slice(tile * LANES, (tile + 1) * LANES)))
    quarter = out_ref.shape[0]

    def taken(some):
        values = [ref[:, at].astype(jnp.float32) for ref, at in some]
        return jnp.concatenate(values, axis=0).astype(jnp.bfloat16)

    groups = [[] for _ in range(toks)]
    at = 0
    for ref, columns in pieces:
        groups[at // quarter].append((ref, columns))
        at += ref.shape[0]
    for tok in range(toks):
        @pl.when(tok_ref[0] == tok)
        def _(tok=tok):
            out_ref[...] = taken(groups[tok])


def pack(shards_in, sections, toks):
    quarter = sum(rows * tiles for _, rows, tiles in sections) // toks
    tok = jnp.zeros((1,), jnp.int32) if toks == 1 else lax.axis_index("tok").astype(jnp.int32)[None]
    return pl.pallas_call(
        functools.partial(pack_kernel, sections, toks),
        out_shape=jax.ShapeDtypeStruct((quarter, LANES), jnp.bfloat16),
        in_specs=[pl.BlockSpec(memory_space=pltpu.SMEM)]
        + [pl.BlockSpec(memory_space=pltpu.VMEM)] * len(shards_in),
        out_specs=pl.BlockSpec(memory_space=pltpu.VMEM),
        name="pack",
    )(tok, *shards_in)


def cycle(count, shift):
    return [(i, (i + shift) % count) for i in range(count)]


def swap_cores(value):
    return lax.ppermute(value, "c", cycle(lax.axis_size("c"), 1))


def start_weights(shards_in):
    packed = jnp.concatenate(
        [
            pack(shards_in[:1], SECTIONS[:1], 1),
            pack(shards_in[1:], SECTIONS[1:], lax.axis_size("tok")),
        ],
        axis=0,
    )
    depth = lax.axis_size("z")
    return jnp.stack(
        [packed]
        + [lax.ppermute(packed, "z", cycle(depth, NEAR * s)) for s in range(1, depth // NEAR)]
    )


def order_weights(far):
    toks, cores, depth = lax.axis_size("tok"), lax.axis_size("c"), lax.axis_size("z")
    tok, core, z = lax.axis_index("tok"), lax.axis_index("c"), lax.axis_index("z")
    steps, packed_rows, lanes = far.shape
    z_low, highs = depth // cores, steps // cores
    twice = jnp.concatenate([far, far])

    def half_for(other):
        first = (z // NEAR - highs * other - (highs - 1)) % steps
        return lax.dynamic_slice_in_dim(twice, first, highs, axis=0)

    both = jnp.stack([half_for(core), swap_cores(half_for(1 - core))])
    near = [both] + [
        lax.ppermute(both, "z", [(i, i // NEAR * NEAR + (i + t) % NEAR) for i in range(depth)])
        for t in range(1, NEAR)
    ]
    count = cores * z_low * packed_rows
    near = jnp.stack(near).reshape(count, lanes)

    def ordered(table, first_row):
        rows, low, from_core = table
        order = ((z - low) % NEAR * cores + (from_core - core) % cores) * highs
        order = (order + highs - 1 - low // NEAR) * packed_rows + first_row + rows
        mover = order[:, None] == jnp.arange(count, dtype=jnp.int32)[None, :]
        return f32_dot(mover.astype(jnp.bfloat16), near).astype(jnp.bfloat16)

    first_table, _, first_rows = row_tables(SECTIONS[:1], 1, z_low, cores)
    rest_table, _, _ = row_tables(SECTIONS[1:], toks, z_low, cores)
    rest = lax.dynamic_index_in_dim(jnp.asarray(rest_table), tok, axis=1, keepdims=False)
    return ordered(jnp.asarray(first_table[:, 0]), 0), ordered(rest, first_rows)


def spread_weights(first, rest):
    groups = lax.axis_size("x")

    def along_x(value):
        return jnp.stack(
            [value] + [lax.ppermute(value, "x", cycle(groups, s)) for s in range(1, groups)]
        )

    rest = along_x(rest)
    first = along_x(first)
    first_other = swap_cores(first)
    left, right = ring_near(rest)
    left, right, first_other = lax.optimization_barrier((left, right, first_other))
    far_low, far_high = ring_far(left, right, 0)
    along_y = jnp.stack([rest, left, jnp.concatenate([far_low, far_high], axis=0), right])
    return assemble(first[None], first_other[None], SECTIONS[:1], 1) + assemble(
        along_y, swap_cores(along_y), SECTIONS[1:], lax.axis_size("tok")
    )


def ring_near(own):
    count = lax.axis_size("tok")
    return lax.ppermute(own, "tok", cycle(count, 1)), lax.ppermute(own, "tok", cycle(count, -1))


def ring_far(left, right, axis):
    count = lax.axis_size("tok")
    half = left.shape[axis] // 2
    low = lax.slice_in_dim(left, 0, half, axis=axis)
    high = lax.slice_in_dim(right, half, 2 * half, axis=axis)
    return lax.ppermute(low, "tok", cycle(count, 1)), lax.ppermute(high, "tok", cycle(count, -1))


def assemble_kernel(places, at_ref, mine_ref, other_ref, *outs):
    toks, groups = mine_ref.shape[:2]
    tok, x, core = at_ref[0], at_ref[1], at_ref[2]
    for out, tiles in zip(outs, places):
        for tile, (place_tok, start, rows) in enumerate(tiles):
            tok_step = lax.rem(tok - place_tok + toks, toks) if toks > 1 else 0
            for x_step in range(groups):
                from_x = lax.rem(x - x_step + groups, groups)
                for source, half in ((mine_ref, core), (other_ref, 1 - core)):
                    out[from_x, half, :, tile * LANES : (tile + 1) * LANES] = source[
                        tok_step, x_step, start : start + rows, :
                    ]


def assemble(mine, other, sections, toks):
    groups = mine.shape[1]
    cores = lax.axis_size("c")
    _, places, _ = row_tables(sections, toks, lax.axis_size("z") // cores, cores)
    place = jnp.stack(
        [lax.axis_index("tok"), lax.axis_index("x"), lax.axis_index("c")]
    ).astype(jnp.int32)
    shapes = [
        jax.ShapeDtypeStruct((groups, cores, tiles[0][2], len(tiles) * LANES), jnp.bfloat16)
        for tiles in places
    ]
    full = pl.pallas_call(
        functools.partial(assemble_kernel, places),
        out_shape=shapes,
        in_specs=[pl.BlockSpec(memory_space=pltpu.SMEM)]
        + [pl.BlockSpec(memory_space=pltpu.VMEM)] * 2,
        out_specs=[pl.BlockSpec(memory_space=pltpu.VMEM)] * len(shapes),
        compiler_params=pltpu.CompilerParams(vmem_limit_bytes=VMEM_BYTES),
        cost_estimate=pl.CostEstimate(
            flops=0, bytes_accessed=4 * mine.size * 2, transcendentals=0
        ),
        name="assemble",
    )(place, mine, other)
    return [matrix.reshape(-1, matrix.shape[-1]) for matrix in full]


def embed_kernel(arrived_ref, matrix_ref, out_ref):
    groups, blocks, images, block_rows, part = arrived_ref.shape
    for image in range(images):
        total = None
        for group in range(groups):
            rows = arrived_ref[group, :, image].astype(jnp.float32)
            rows = rows.reshape(blocks * block_rows, part).astype(jnp.bfloat16)
            product = f32_dot(rows, matrix_ref[group * part : (group + 1) * part, :])
            total = product if total is None else total + product
        out_ref[image] = total.astype(jnp.bfloat16)


def embed(arrived, matrix):
    groups, blocks, images, block_rows, part = arrived.shape
    rows, width = blocks * block_rows, matrix.shape[1]
    return pl.pallas_call(
        embed_kernel,
        out_shape=jax.ShapeDtypeStruct((images, rows, width), jnp.bfloat16),
        compiler_params=pltpu.CompilerParams(vmem_limit_bytes=VMEM_BYTES),
        cost_estimate=pl.CostEstimate(
            flops=2 * images * rows * matrix.size,
            bytes_accessed=2 * (arrived.size + matrix.size + images * rows * width),
            transcendentals=0,
        ),
        name="embed",
    )(arrived, matrix)


def head_halves():
    return lax.broadcasted_iota(jnp.int32, (1, LANES), 1) < HD


def fold(queries, key_ref, value_ref, first_key, first_value, totals, chunk=256):
    others = key_ref.shape[0]
    low_half = head_halves()
    across = (((1,), (1,)), ((), ()))
    done = []
    for pair in range(HEADS // 2):
        query = queries[:, pair * LANES : (pair + 1) * LANES]
        blank = jnp.zeros_like(query)
        low_query = jnp.where(low_half, query, blank)
        high_query = jnp.where(low_half, blank, query)
        low_total, high_total = totals[2 * pair], totals[2 * pair + 1]
        for start in range(0, others, chunk):
            at = slice(start, start + chunk)
            keys = key_ref[at, first_key + pair * LANES : first_key + (pair + 1) * LANES]
            values = value_ref[at, first_value + pair * LANES : first_value + (pair + 1) * LANES]
            ones = jnp.ones_like(values)
            scores = lax.dot_general(low_query, keys, across, preferred_element_type=jnp.float32)
            weights = jnp.exp(scores).astype(jnp.bfloat16)
            low_total = low_total + f32_dot(weights, jnp.where(low_half, values, ones))
            scores = lax.dot_general(high_query, keys, across, preferred_element_type=jnp.float32)
            weights = jnp.exp(scores).astype(jnp.bfloat16)
            high_total = high_total + f32_dot(weights, jnp.where(low_half, ones, values))
        done += [low_total, high_total]
    return done


def finish(totals):
    low_half = head_halves()
    done = []
    for pair in range(HEADS // 2):
        low_total, high_total = totals[2 * pair], totals[2 * pair + 1]
        numer = jnp.where(low_half, low_total, high_total)
        denom = pltpu.roll(jnp.where(low_half, high_total, low_total), HD, 1)
        done.append((numer / denom).astype(jnp.bfloat16))
    return jnp.concatenate(done, axis=1)


def nothing(rows):
    return [jnp.zeros((rows, LANES), jnp.float32)] * HEADS


def scaled(queries):
    return (queries.astype(jnp.bfloat16).astype(jnp.float32) * HD**-0.5).astype(jnp.bfloat16)


def self_kernel(first, last, pieces, *refs):
    refs = list(refs)
    piece_refs = [refs.pop(0) for _ in range(pieces)]
    if not first:
        query_ref, totals_in = refs.pop(0), refs.pop(0)
    if last:
        own_ref = refs.pop(0)
    project_ref, keyval_ref = refs.pop(0), refs.pop(0)
    width = keyval_ref.shape[1] // 2
    if last:
        output_ref, second_ref = refs.pop(0), refs.pop(0)
    cross_ref = refs.pop(0)
    if first:
        query_out = refs.pop(0)
    if last:
        after_ref, next_ref = refs.pop(0), refs.pop(0)
    else:
        totals_out = refs.pop(0)
    scratch = refs.pop(0)
    at = 0
    for ref in piece_refs:
        normed = normalize(ref[0].astype(jnp.float32)).astype(jnp.bfloat16)
        here = slice(at, at + normed.shape[0])
        scratch[here] = f32_dot(normed, project_ref[:, width:]).astype(jnp.bfloat16)
        cross_ref[0, here] = f32_dot(normed, keyval_ref[...]).astype(jnp.bfloat16)
        at += normed.shape[0]
    if first:
        queries = scaled(f32_dot(normed, project_ref[:, :width]))
        query_out[0] = queries
        totals = nothing(queries.shape[0])
    else:
        queries = query_ref[0]
        totals = [totals_in[0, head] for head in range(HEADS)]
    totals = fold(queries, scratch, scratch, 0, width, totals)
    if last:
        after = own_ref[0].astype(jnp.float32) + f32_dot(finish(totals), output_ref[...])
        after_ref[0] = after
        second = normalize(after).astype(jnp.bfloat16)
        next_ref[0] = scaled(f32_dot(second, second_ref[...]))
    else:
        for head in range(HEADS):
            totals_out[0, head] = totals[head]


def per_image(shape):
    return pl.BlockSpec((1,) + shape[1:], lambda i: (i,) + (0,) * (len(shape) - 1))


def whole(matrix):
    return pl.BlockSpec(matrix.shape, lambda i: (0, 0))


def self_step(pieces, project, keyval, carry=None, ending=None):
    first, last = carry is None, ending is not None
    images, _, model = pieces[0].shape
    width = keyval.shape[1] // 2
    others = sum(piece.shape[1] for piece in pieces)
    arrays = list(pieces) + list(carry or ())
    matrices = [project, keyval]
    if last:
        arrays.append(ending[0])
        matrices += ending[1:]
    rows = pieces[0].shape[1] if first else carry[0].shape[1]
    shapes = [jax.ShapeDtypeStruct((images, others, 2 * width), jnp.bfloat16)]
    if first:
        shapes.append(jax.ShapeDtypeStruct((images, rows, width), jnp.bfloat16))
    if last:
        shapes.append(jax.ShapeDtypeStruct((images, rows, model), jnp.float32))
        shapes.append(jax.ShapeDtypeStruct((images, rows, width), jnp.bfloat16))
    else:
        shapes.append(jax.ShapeDtypeStruct((images, HEADS, rows, LANES), jnp.float32))
    return pl.pallas_call(
        functools.partial(self_kernel, first, last, len(pieces)),
        grid=(images,),
        out_shape=shapes,
        in_specs=[per_image(array.shape) for array in arrays] + [whole(matrix) for matrix in matrices],
        out_specs=[per_image(shape.shape) for shape in shapes],
        scratch_shapes=[pltpu.VMEM((others, 2 * width), jnp.bfloat16)],
        compiler_params=pltpu.CompilerParams(vmem_limit_bytes=VMEM_BYTES),
        cost_estimate=pl.CostEstimate(
            flops=2 * images * (others * model * 4 * width + 4 * rows * others * width),
            bytes_accessed=2 * sum(matrix.size for matrix in matrices)
            + sum(array.size * array.dtype.itemsize for array in arrays),
            transcendentals=images * HEADS * rows * others,
        ),
        name="self_step",
    )(*arrays, *matrices)


def cross_kernel(pieces, after_ref, query_ref, *refs):
    keyval_refs, output_ref, out_ref = refs[:pieces], refs[pieces], refs[pieces + 1]
    width = output_ref.shape[0]
    halves, blocks, block_rows, part = out_ref.shape[1:]
    queries = query_ref[0]
    totals = nothing(queries.shape[0])
    for ref in keyval_refs:
        keyval = ref.at[0]
        totals = fold(queries, keyval, keyval, 0, width, totals)
    mixed = after_ref[0] + f32_dot(finish(totals), output_ref[...])
    for half in range(halves):
        columns = mixed[:, half * part : (half + 1) * part]
        out_ref[0, half] = columns.reshape(blocks, block_rows, part).astype(jnp.bfloat16)


def cross_block(after, query, keyvals, output, halves, block_rows):
    images, rows, model = after.shape
    width = output.shape[0]
    everyone = sum(keyval.shape[1] for keyval in keyvals)
    shape = (images, halves, rows // block_rows, block_rows, model // halves)
    return pl.pallas_call(
        functools.partial(cross_kernel, len(keyvals)),
        grid=(images,),
        out_shape=jax.ShapeDtypeStruct(shape, jnp.bfloat16),
        in_specs=[per_image(after.shape), per_image(query.shape)]
        + [
            pl.BlockSpec((1,) + keyval.shape[1:], lambda i: (images - 1 - i, 0, 0))
            for keyval in keyvals
        ]
        + [whole(output)],
        out_specs=per_image(shape),
        compiler_params=pltpu.CompilerParams(vmem_limit_bytes=VMEM_BYTES),
        cost_estimate=pl.CostEstimate(
            flops=2 * images * (4 * rows * everyone * width + rows * model * width),
            bytes_accessed=4 * after.size + 2 * (query.size + output.size + after.size),
            transcendentals=images * HEADS * rows * everyone,
        ),
        name="cross_block",
    )(after, query, *keyvals, output)


def shards(tokens, pair_list, owner_base, *weight_shards):
    groups = lax.axis_size("x")
    row_devices = lax.axis_size("z") * lax.axis_size("c")
    devices = groups * row_devices
    column = lax.axis_index("z") * lax.axis_size("c") + lax.axis_index("c")
    spread, block_rows, encoder = tokens.shape[1], tokens.shape[3], tokens.shape[4]
    held = tokens.reshape(spread, block_rows, encoder)
    part = encoder // groups

    parted = jnp.stack([held[:, :, x * part : (x + 1) * part] for x in range(groups)])
    parted, weight_shards = lax.optimization_barrier((parted, weight_shards))
    pieces = lax.all_to_all(parted, "x", 0, 0, tiled=True).reshape(devices, block_rows, part)
    far = start_weights(weight_shards)

    bases = owner_base[pair_list]
    slot = (column - bases) % spread
    source = ((bases + slot - column) // row_devices) % groups
    place = source * spread + slot
    outgoing = jnp.take(pieces, place.reshape(-1), axis=0, mode="clip").reshape(
        devices, 2, block_rows, part
    )
    outgoing, far = lax.optimization_barrier((outgoing, far))
    arrived = lax.all_to_all(outgoing, IMG, 0, 0, tiled=True)
    arrived = arrived.reshape(groups, row_devices, 2, block_rows, part)
    full = spread_weights(*order_weights(far))
    embed_full, project_full, self_out_full, query_full, keyval_full, cross_out_full = full
    model_width = embed_full.shape[1]

    embedded = embed(arrived, embed_full)
    left, right = ring_near(embedded)
    near_keyval, queries, totals = self_step([embedded], project_full, keyval_full)
    left, right, totals = lax.optimization_barrier((left, right, totals))
    far_low, far_high = ring_far(left, right, 1)
    next_keyval, totals = self_step([left, right], project_full, keyval_full, (queries, totals))
    far_keyval, after_self, cross_queries = self_step(
        [far_low, far_high], project_full, keyval_full, (queries, totals),
        (embedded, self_out_full, query_full),
    )

    halves = groups // 2
    backward = cross_block(
        after_self, cross_queries, [near_keyval, next_keyval, far_keyval], cross_out_full,
        halves, block_rows,
    ).reshape(devices, block_rows, model_width // halves)
    returned = lax.all_to_all(backward, IMG, 0, 0, tiled=True)
    my_half = lax.axis_index("x") // halves
    my_place = lax.dynamic_index_in_dim(place, my_half, axis=1, keepdims=False)
    selector = (
        my_place[None, :] == jnp.arange(devices, dtype=jnp.int32)[:, None]
    ).astype(jnp.bfloat16)
    partial = jnp.einsum(
        "ge,ebd->gbd", selector, returned, preferred_element_type=jnp.float32
    ).astype(jnp.bfloat16)
    home = lax.all_to_all(
        partial.reshape(groups, spread, block_rows, model_width // halves), "x", 0, 0, tiled=True
    )
    home = home.reshape(2, halves, spread, block_rows, model_width // halves)
    total = home[0].astype(jnp.float32) + home[1].astype(jnp.float32)
    summed = jnp.concatenate([total[half] for half in range(halves)], axis=-1)
    return summed.astype(jnp.bfloat16).reshape(1, spread, 1, block_rows, model_width)


def solution(mesh):
    chips = Mesh(mesh.devices.reshape(4, 16, 2, 4), ("x", "z", "c", "tok"))
    rows = P(IMG, None)
    tokens = P(IMG, None, "tok", None, None)
    return jax.shard_map(
        shards,
        mesh=chips,
        in_specs=(tokens, P(), P()) + (rows,) * 6,
        out_specs=tokens,
        check_vma=False,
    )
```

```python
import functools

import jax
import jax.numpy as jnp
import numpy as np
from jax import lax
from jax.experimental import pallas as pl
from jax.experimental.pallas import tpu as pltpu
from jax.sharding import Mesh, PartitionSpec as P

HEADS = 6
HD = 64
LANES = 128
IMG = ("x", "z", "c")
NEAR = 4
VMEM_BYTES = 50 * 1024 * 1024

SECTIONS = (
    ("embed", 8, 6),
    ("project", 6, 9),
    ("self_out", 3, 6),
    ("query", 6, 3),
    ("keyval", 6, 6),
    ("cross_out", 3, 6),
)
def f32_dot(left, right):
    return jnp.dot(left, right, preferred_element_type=jnp.float32)


def normalize(values):
    mean_value = jnp.mean(values, axis=-1, keepdims=True)
    centred = values - mean_value
    variance = jnp.mean(centred * centred, axis=-1, keepdims=True)
    return centred * lax.rsqrt(variance + 1e-06)


def row_tables(sections, toks, z_low, cores):
    total = sum(rows * tiles for _, rows, tiles in sections)
    quarter = total // toks
    table = np.zeros((3, toks, quarter * z_low * cores), np.int32)
    places = []
    at = 0
    for _, rows, tiles in sections:
        places.append([])
        for _ in range(tiles):
            tok, start = divmod(at, quarter)
            assert start + rows <= quarter
            out = start * z_low * cores
            places[-1].append((tok, out, rows * z_low * cores))
            for z in range(z_low):
                for core in range(cores):
                    for row in range(rows):
                        table[:, tok, out] = (start + row, z, core)
                        out += 1
            at += rows
    return table, places, quarter


def pack_kernel(sections, toks, tok_ref, *refs):
    shard_refs, out_ref = refs[:-1], refs[-1]
    pieces = []
    for ref, (_, _, tiles) in zip(shard_refs, sections):
        for tile in range(tiles):
            pieces.append((ref, slice(tile * LANES, (tile + 1) * LANES)))
    quarter = out_ref.shape[0]

    def taken(some):
        values = [ref[:, at].astype(jnp.float32) for ref, at in some]
        return jnp.concatenate(values, axis=0).astype(jnp.bfloat16)

    groups = [[] for _ in range(toks)]
    at = 0
    for ref, columns in pieces:
        groups[at // quarter].append((ref, columns))
        at += ref.shape[0]
    for tok in range(toks):
        @pl.when(tok_ref[0] == tok)
        def _(tok=tok):
            out_ref[...] = taken(groups[tok])


def pack(shards_in, sections, toks):
    quarter = sum(rows * tiles for _, rows, tiles in sections) // toks
    tok = jnp.zeros((1,), jnp.int32) if toks == 1 else lax.axis_index("tok").astype(jnp.int32)[None]
    return pl.pallas_call(
        functools.partial(pack_kernel, sections, toks),
        out_shape=jax.ShapeDtypeStruct((quarter, LANES), jnp.bfloat16),
        in_specs=[pl.BlockSpec(memory_space=pltpu.SMEM)]
        + [pl.BlockSpec(memory_space=pltpu.VMEM)] * len(shards_in),
        out_specs=pl.BlockSpec(memory_space=pltpu.VMEM),
        name="pack",
    )(tok, *shards_in)


def cycle(count, shift):
    return [(i, (i + shift) % count) for i in range(count)]


def swap_cores(value):
    return lax.ppermute(value, "c", cycle(lax.axis_size("c"), 1))


def start_weights(shards_in):
    packed = jnp.concatenate(
        [
            pack(shards_in[:1], SECTIONS[:1], 1),
            pack(shards_in[1:], SECTIONS[1:], lax.axis_size("tok")),
        ],
        axis=0,
    )
    depth = lax.axis_size("z")
    return jnp.stack(
        [packed]
        + [lax.ppermute(packed, "z", cycle(depth, NEAR * s)) for s in range(1, depth // NEAR)]
    )


def near_weights(far):
    cores, depth = lax.axis_size("c"), lax.axis_size("z")
    core, z = lax.axis_index("c"), lax.axis_index("z")
    steps = far.shape[0]
    highs = steps // cores
    twice = jnp.concatenate([far, far])

    def half_for(other):
        first = (z // NEAR - highs * other - (highs - 1)) % steps
        return lax.dynamic_slice_in_dim(twice, first, highs, axis=0)

    both = jnp.stack([half_for(core), swap_cores(half_for(1 - core))])
    near = [both] + [
        lax.ppermute(both, "z", [(i, i // NEAR * NEAR + (i + t) % NEAR) for i in range(depth)])
        for t in range(1, NEAR)
    ]
    return jnp.stack(near)


def order_weights(near):
    toks, cores, depth = lax.axis_size("tok"), lax.axis_size("c"), lax.axis_size("z")
    tok, core, z = lax.axis_index("tok"), lax.axis_index("c"), lax.axis_index("z")
    _, _, highs, packed_rows, lanes = near.shape
    z_low = depth // cores
    count = cores * z_low * packed_rows
    near = near.reshape(count, lanes)

    first_table, _, first_rows = row_tables(SECTIONS[:1], 1, z_low, cores)
    rest_table, _, _ = row_tables(SECTIONS[1:], toks, z_low, cores)
    rest = lax.dynamic_index_in_dim(jnp.asarray(rest_table), tok, axis=1, keepdims=False)
    rest = rest + jnp.asarray([[first_rows], [0], [0]], jnp.int32)
    rows, low, from_core = jnp.concatenate([jnp.asarray(first_table[:, 0]), rest], axis=1)
    order = ((z - low) % NEAR * cores + (from_core - core) % cores) * highs
    order = (order + highs - 1 - low // NEAR) * packed_rows + rows
    mover = order[:, None] == jnp.arange(count, dtype=jnp.int32)[None, :]
    ordered = f32_dot(mover.astype(jnp.bfloat16), near).astype(jnp.bfloat16)
    return ordered, first_table.shape[2]


def spread_weights(ordered, first_rows):
    left, right = near_on_ring(ordered, "x")
    far_first = pass_on(left[:first_rows], "x", 1)
    far_rest = pass_on(right[first_rows:], "x", -1)
    first = jnp.stack([ordered[:first_rows], left[:first_rows], far_first, right[:first_rows]])
    rest = jnp.stack([ordered[first_rows:], left[first_rows:], far_rest, right[first_rows:]])
    first_other = swap_cores(first)
    left, right = near_on_ring(rest, "tok")
    left, right, first_other = lax.optimization_barrier((left, right, first_other))
    far_low, far_high = ring_far(left, right, 0)
    along_y = jnp.stack([rest, left, jnp.concatenate([far_low, far_high], axis=0), right])
    return assemble(first[None], first_other[None], SECTIONS[:1], 1) + assemble(
        along_y, swap_cores(along_y), SECTIONS[1:], lax.axis_size("tok")
    )


def pass_on(value, axis, shift):
    return lax.ppermute(value, axis, cycle(lax.axis_size(axis), shift))


def near_on_ring(own, axis):
    return pass_on(own, axis, 1), pass_on(own, axis, -1)


def ring_far(left, right, axis):
    half = left.shape[axis] // 2
    low = lax.slice_in_dim(left, 0, half, axis=axis)
    high = lax.slice_in_dim(right, half, 2 * half, axis=axis)
    return pass_on(low, "tok", 1), pass_on(high, "tok", -1)


def assemble_kernel(places, at_ref, mine_ref, other_ref, *outs):
    toks, groups = mine_ref.shape[:2]
    tok, x, core = at_ref[0], at_ref[1], at_ref[2]
    for out, tiles in zip(outs, places):
        for tile, (place_tok, start, rows) in enumerate(tiles):
            tok_step = lax.rem(tok - place_tok + toks, toks) if toks > 1 else 0
            for x_step in range(groups):
                from_x = lax.rem(x - x_step + groups, groups)
                for source, half in ((mine_ref, core), (other_ref, 1 - core)):
                    out[from_x, half, :, tile * LANES : (tile + 1) * LANES] = source[
                        tok_step, x_step, start : start + rows, :
                    ]


def assemble(mine, other, sections, toks):
    groups = mine.shape[1]
    cores = lax.axis_size("c")
    _, places, _ = row_tables(sections, toks, lax.axis_size("z") // cores, cores)
    place = jnp.stack(
        [lax.axis_index("tok"), lax.axis_index("x"), lax.axis_index("c")]
    ).astype(jnp.int32)
    shapes = [
        jax.ShapeDtypeStruct((groups, cores, tiles[0][2], len(tiles) * LANES), jnp.bfloat16)
        for tiles in places
    ]
    full = pl.pallas_call(
        functools.partial(assemble_kernel, places),
        out_shape=shapes,
        in_specs=[pl.BlockSpec(memory_space=pltpu.SMEM)]
        + [pl.BlockSpec(memory_space=pltpu.VMEM)] * 2,
        out_specs=[pl.BlockSpec(memory_space=pltpu.VMEM)] * len(shapes),
        compiler_params=pltpu.CompilerParams(vmem_limit_bytes=VMEM_BYTES),
        cost_estimate=pl.CostEstimate(
            flops=0, bytes_accessed=4 * mine.size * 2, transcendentals=0
        ),
        name="assemble",
    )(place, mine, other)
    return [matrix.reshape(-1, matrix.shape[-1]) for matrix in full]


def embed_kernel(arrived_ref, matrix_ref, out_ref):
    groups, blocks, images, block_rows, part = arrived_ref.shape
    for image in range(images):
        total = None
        for group in range(groups):
            rows = arrived_ref[group, :, image].astype(jnp.float32)
            rows = rows.reshape(blocks * block_rows, part).astype(jnp.bfloat16)
            product = f32_dot(rows, matrix_ref[group * part : (group + 1) * part, :])
            total = product if total is None else total + product
        out_ref[image] = total.astype(jnp.bfloat16)


def embed(arrived, matrix):
    groups, blocks, images, block_rows, part = arrived.shape
    rows, width = blocks * block_rows, matrix.shape[1]
    return pl.pallas_call(
        embed_kernel,
        out_shape=jax.ShapeDtypeStruct((images, rows, width), jnp.bfloat16),
        compiler_params=pltpu.CompilerParams(vmem_limit_bytes=VMEM_BYTES),
        cost_estimate=pl.CostEstimate(
            flops=2 * images * rows * matrix.size,
            bytes_accessed=2 * (arrived.size + matrix.size + images * rows * width),
            transcendentals=0,
        ),
        name="embed",
    )(arrived, matrix)


def head_halves():
    return lax.broadcasted_iota(jnp.int32, (1, LANES), 1) < HD


def fold(queries, key_ref, value_ref, first_key, first_value, totals, chunk=256):
    others = key_ref.shape[0]
    low_half = head_halves()
    across = (((1,), (1,)), ((), ()))
    done = []
    for pair in range(HEADS // 2):
        query = queries[:, pair * LANES : (pair + 1) * LANES]
        blank = jnp.zeros_like(query)
        low_query = jnp.where(low_half, query, blank)
        high_query = jnp.where(low_half, blank, query)
        low_total, high_total = totals[2 * pair], totals[2 * pair + 1]
        for start in range(0, others, chunk):
            at = slice(start, start + chunk)
            keys = key_ref[at, first_key + pair * LANES : first_key + (pair + 1) * LANES]
            values = value_ref[at, first_value + pair * LANES : first_value + (pair + 1) * LANES]
            ones = jnp.ones_like(values)
            scores = lax.dot_general(low_query, keys, across, preferred_element_type=jnp.float32)
            weights = jnp.exp(scores).astype(jnp.bfloat16)
            low_total = low_total + f32_dot(weights, jnp.where(low_half, values, ones))
            scores = lax.dot_general(high_query, keys, across, preferred_element_type=jnp.float32)
            weights = jnp.exp(scores).astype(jnp.bfloat16)
            high_total = high_total + f32_dot(weights, jnp.where(low_half, ones, values))
        done += [low_total, high_total]
    return done


def finish(totals):
    low_half = head_halves()
    done = []
    for pair in range(HEADS // 2):
        low_total, high_total = totals[2 * pair], totals[2 * pair + 1]
        numer = jnp.where(low_half, low_total, high_total)
        denom = pltpu.roll(jnp.where(low_half, high_total, low_total), HD, 1)
        done.append((numer / denom).astype(jnp.bfloat16))
    return jnp.concatenate(done, axis=1)


def nothing(rows):
    return [jnp.zeros((rows, LANES), jnp.float32)] * HEADS


def scaled(queries):
    return (queries.astype(jnp.bfloat16).astype(jnp.float32) * HD**-0.5).astype(jnp.bfloat16)


def self_kernel(first, last, pieces, *refs):
    refs = list(refs)
    piece_refs = [refs.pop(0) for _ in range(pieces)]
    if not first:
        query_ref, totals_in = refs.pop(0), refs.pop(0)
    if last:
        own_ref = refs.pop(0)
    project_ref, keyval_ref = refs.pop(0), refs.pop(0)
    width = keyval_ref.shape[1] // 2
    if last:
        output_ref, second_ref = refs.pop(0), refs.pop(0)
    cross_ref = refs.pop(0)
    if first:
        query_out = refs.pop(0)
    if last:
        after_ref, next_ref = refs.pop(0), refs.pop(0)
    else:
        totals_out = refs.pop(0)
    scratch = refs.pop(0)
    at = 0
    for ref in piece_refs:
        normed = normalize(ref[0].astype(jnp.float32)).astype(jnp.bfloat16)
        here = slice(at, at + normed.shape[0])
        scratch[here] = f32_dot(normed, project_ref[:, width:]).astype(jnp.bfloat16)
        cross_ref[0, here] = f32_dot(normed, keyval_ref[...]).astype(jnp.bfloat16)
        at += normed.shape[0]
    if first:
        queries = scaled(f32_dot(normed, project_ref[:, :width]))
        query_out[0] = queries
        totals = nothing(queries.shape[0])
    else:
        queries = query_ref[0]
        totals = [totals_in[0, head] for head in range(HEADS)]
    totals = fold(queries, scratch, scratch, 0, width, totals)
    if last:
        after = own_ref[0].astype(jnp.float32) + f32_dot(finish(totals), output_ref[...])
        after_ref[0] = after
        second = normalize(after).astype(jnp.bfloat16)
        next_ref[0] = scaled(f32_dot(second, second_ref[...]))
    else:
        for head in range(HEADS):
            totals_out[0, head] = totals[head]


def per_image(shape):
    return pl.BlockSpec((1,) + shape[1:], lambda i: (i,) + (0,) * (len(shape) - 1))


def whole(matrix):
    return pl.BlockSpec(matrix.shape, lambda i: (0, 0))


def self_step(pieces, project, keyval, carry=None, ending=None):
    first, last = carry is None, ending is not None
    images, _, model = pieces[0].shape
    width = keyval.shape[1] // 2
    others = sum(piece.shape[1] for piece in pieces)
    arrays = list(pieces) + list(carry or ())
    matrices = [project, keyval]
    if last:
        arrays.append(ending[0])
        matrices += ending[1:]
    rows = pieces[0].shape[1] if first else carry[0].shape[1]
    shapes = [jax.ShapeDtypeStruct((images, others, 2 * width), jnp.bfloat16)]
    if first:
        shapes.append(jax.ShapeDtypeStruct((images, rows, width), jnp.bfloat16))
    if last:
        shapes.append(jax.ShapeDtypeStruct((images, rows, model), jnp.float32))
        shapes.append(jax.ShapeDtypeStruct((images, rows, width), jnp.bfloat16))
    else:
        shapes.append(jax.ShapeDtypeStruct((images, HEADS, rows, LANES), jnp.float32))
    return pl.pallas_call(
        functools.partial(self_kernel, first, last, len(pieces)),
        grid=(images,),
        out_shape=shapes,
        in_specs=[per_image(array.shape) for array in arrays] + [whole(matrix) for matrix in matrices],
        out_specs=[per_image(shape.shape) for shape in shapes],
        scratch_shapes=[pltpu.VMEM((others, 2 * width), jnp.bfloat16)],
        compiler_params=pltpu.CompilerParams(vmem_limit_bytes=VMEM_BYTES),
        cost_estimate=pl.CostEstimate(
            flops=2 * images * (others * model * 4 * width + 4 * rows * others * width),
            bytes_accessed=2 * sum(matrix.size for matrix in matrices)
            + sum(array.size * array.dtype.itemsize for array in arrays),
            transcendentals=images * HEADS * rows * others,
        ),
        name="self_step",
    )(*arrays, *matrices)


def cross_kernel(pieces, after_ref, query_ref, *refs):
    keyval_refs, output_ref, out_ref = refs[:pieces], refs[pieces], refs[pieces + 1]
    width = output_ref.shape[0]
    halves, blocks, block_rows, part = out_ref.shape[1:]
    queries = query_ref[0]
    totals = nothing(queries.shape[0])
    for ref in keyval_refs:
        keyval = ref.at[0]
        totals = fold(queries, keyval, keyval, 0, width, totals)
    mixed = after_ref[0] + f32_dot(finish(totals), output_ref[...])
    for half in range(halves):
        columns = mixed[:, half * part : (half + 1) * part]
        out_ref[0, half] = columns.reshape(blocks, block_rows, part).astype(jnp.bfloat16)


def cross_block(after, query, keyvals, output, halves, block_rows):
    images, rows, model = after.shape
    width = output.shape[0]
    everyone = sum(keyval.shape[1] for keyval in keyvals)
    shape = (images, halves, rows // block_rows, block_rows, model // halves)
    return pl.pallas_call(
        functools.partial(cross_kernel, len(keyvals)),
        grid=(images,),
        out_shape=jax.ShapeDtypeStruct(shape, jnp.bfloat16),
        in_specs=[per_image(after.shape), per_image(query.shape)]
        + [
            pl.BlockSpec((1,) + keyval.shape[1:], lambda i: (images - 1 - i, 0, 0))
            for keyval in keyvals
        ]
        + [whole(output)],
        out_specs=per_image(shape),
        compiler_params=pltpu.CompilerParams(vmem_limit_bytes=VMEM_BYTES),
        cost_estimate=pl.CostEstimate(
            flops=2 * images * (4 * rows * everyone * width + rows * model * width),
            bytes_accessed=4 * after.size + 2 * (query.size + output.size + after.size),
            transcendentals=images * HEADS * rows * everyone,
        ),
        name="cross_block",
    )(after, query, *keyvals, output)


def shards(tokens, pair_list, owner_base, *weight_shards):
    groups = lax.axis_size("x")
    row_devices = lax.axis_size("z") * lax.axis_size("c")
    devices = groups * row_devices
    column = lax.axis_index("z") * lax.axis_size("c") + lax.axis_index("c")
    spread, block_rows, encoder = tokens.shape[1], tokens.shape[3], tokens.shape[4]
    held = tokens.reshape(spread, block_rows, encoder)
    part = encoder // groups

    parted = jnp.stack([held[:, :, x * part : (x + 1) * part] for x in range(groups)])
    parted, weight_shards = lax.optimization_barrier((parted, weight_shards))
    pieces = lax.all_to_all(parted, "x", 0, 0, tiled=True).reshape(devices, block_rows, part)
    far = start_weights(weight_shards)

    bases = owner_base[pair_list]
    slot = (column - bases) % spread
    source = ((bases + slot - column) // row_devices) % groups
    place = source * spread + slot
    outgoing = jnp.take(pieces, place.reshape(-1), axis=0, mode="clip").reshape(
        devices, 2, block_rows, part
    )
    outgoing, near = lax.optimization_barrier((outgoing, near_weights(far)))
    arrived = lax.all_to_all(outgoing, IMG, 0, 0, tiled=True)
    arrived = arrived.reshape(groups, row_devices, 2, block_rows, part)
    full = spread_weights(*order_weights(near))
    embed_full, project_full, self_out_full, query_full, keyval_full, cross_out_full = full
    model_width = embed_full.shape[1]

    embedded = embed(arrived, embed_full)
    left, right = near_on_ring(embedded, "tok")
    near_keyval, queries, totals = self_step([embedded], project_full, keyval_full)
    left, right, totals = lax.optimization_barrier((left, right, totals))
    far_low, far_high = ring_far(left, right, 1)
    next_keyval, totals = self_step([left, right], project_full, keyval_full, (queries, totals))
    far_keyval, after_self, cross_queries = self_step(
        [far_low, far_high], project_full, keyval_full, (queries, totals),
        (embedded, self_out_full, query_full),
    )

    halves = groups // 2
    backward = cross_block(
        after_self, cross_queries, [near_keyval, next_keyval, far_keyval], cross_out_full,
        halves, block_rows,
    ).reshape(devices, block_rows, model_width // halves)
    returned = lax.all_to_all(backward, IMG, 0, 0, tiled=True)
    my_half = lax.axis_index("x") // halves
    my_place = lax.dynamic_index_in_dim(place, my_half, axis=1, keepdims=False)
    selector = (
        my_place[None, :] == jnp.arange(devices, dtype=jnp.int32)[:, None]
    ).astype(jnp.bfloat16)
    partial = jnp.einsum(
        "ge,ebd->gbd", selector, returned, preferred_element_type=jnp.float32
    ).astype(jnp.bfloat16)
    home = lax.all_to_all(
        partial.reshape(groups, spread, block_rows, model_width // halves), "x", 0, 0, tiled=True
    )
    home = home.reshape(2, halves, spread, block_rows, model_width // halves)
    total = home[0].astype(jnp.float32) + home[1].astype(jnp.float32)
    summed = jnp.concatenate([total[half] for half in range(halves)], axis=-1)
    return summed.astype(jnp.bfloat16).reshape(1, spread, 1, block_rows, model_width)


def solution(mesh):
    chips = Mesh(mesh.devices.reshape(4, 16, 2, 4), ("x", "z", "c", "tok"))
    rows = P(IMG, None)
    tokens = P(IMG, None, "tok", None, None)
    return jax.shard_map(
        shards,
        mesh=chips,
        in_specs=(tokens, P(), P()) + (rows,) * 6,
        out_specs=tokens,
        check_vma=False,
    )
```

```python
import functools

import jax
import jax.numpy as jnp
import numpy as np
from jax import lax
from jax.experimental import pallas as pl
from jax.experimental.pallas import tpu as pltpu
from jax.sharding import Mesh, PartitionSpec as P

HEADS = 6
HD = 64
LANES = 128
IMG = ("x", "z", "c")
VMEM_BYTES = 50 * 1024 * 1024

SECTIONS = (
    ("embed", 8, 6),
    ("project", 6, 9),
    ("self_out", 3, 6),
    ("query", 6, 3),
    ("keyval", 6, 6),
    ("cross_out", 3, 6),
)
def f32_dot(left, right):
    return jnp.dot(left, right, preferred_element_type=jnp.float32)


def normalize(values):
    mean_value = jnp.mean(values, axis=-1, keepdims=True)
    centred = values - mean_value
    variance = jnp.mean(centred * centred, axis=-1, keepdims=True)
    return centred * lax.rsqrt(variance + 1e-06)


def row_tables(sections, toks, z_low, cores):
    total = sum(rows * tiles for _, rows, tiles in sections)
    quarter = total // toks
    table = np.zeros((3, toks, quarter * z_low * cores), np.int32)
    places = []
    at = 0
    for _, rows, tiles in sections:
        places.append([])
        for _ in range(tiles):
            tok, start = divmod(at, quarter)
            assert start + rows <= quarter
            out = start * z_low * cores
            places[-1].append((tok, out, rows * z_low * cores))
            for z in range(z_low):
                for core in range(cores):
                    for row in range(rows):
                        table[:, tok, out] = (start + row, z, core)
                        out += 1
            at += rows
    return table, places, quarter


def pack_kernel(sections, toks, tok_ref, *refs):
    shard_refs, out_ref = refs[:-1], refs[-1]
    pieces = []
    for ref, (_, _, tiles) in zip(shard_refs, sections):
        for tile in range(tiles):
            pieces.append((ref, slice(tile * LANES, (tile + 1) * LANES)))
    quarter = out_ref.shape[0]

    def taken(some):
        values = [ref[:, at].astype(jnp.float32) for ref, at in some]
        return jnp.concatenate(values, axis=0).astype(jnp.bfloat16)

    groups = [[] for _ in range(toks)]
    at = 0
    for ref, columns in pieces:
        groups[at // quarter].append((ref, columns))
        at += ref.shape[0]
    for tok in range(toks):
        @pl.when(tok_ref[0] == tok)
        def _(tok=tok):
            out_ref[...] = taken(groups[tok])


def pack(shards_in, sections, toks):
    quarter = sum(rows * tiles for _, rows, tiles in sections) // toks
    tok = jnp.zeros((1,), jnp.int32) if toks == 1 else lax.axis_index("tok").astype(jnp.int32)[None]
    return pl.pallas_call(
        functools.partial(pack_kernel, sections, toks),
        out_shape=jax.ShapeDtypeStruct((quarter, LANES), jnp.bfloat16),
        in_specs=[pl.BlockSpec(memory_space=pltpu.SMEM)]
        + [pl.BlockSpec(memory_space=pltpu.VMEM)] * len(shards_in),
        out_specs=pl.BlockSpec(memory_space=pltpu.VMEM),
        name="pack",
    )(tok, *shards_in)


def cycle(count, shift):
    return [(i, (i + shift) % count) for i in range(count)]


def swap_cores(value):
    return lax.ppermute(value, "c", cycle(lax.axis_size("c"), 1))


def start_weights(shards_in):
    packed = jnp.concatenate(
        [
            pack(shards_in[:1], SECTIONS[:1], 1),
            pack(shards_in[1:], SECTIONS[1:], lax.axis_size("tok")),
        ],
        axis=0,
    )
    copies = jnp.broadcast_to(packed[None], (lax.axis_size("z"),) + packed.shape)
    return lax.all_to_all(copies, "z", 0, 0, tiled=True)


def order_weights(along_z):
    toks, cores, depth = lax.axis_size("tok"), lax.axis_size("c"), lax.axis_size("z")
    tok, core = lax.axis_index("tok"), lax.axis_index("c")
    _, packed_rows, lanes = along_z.shape
    z_low = depth // cores
    count = cores * z_low * packed_rows
    mine = lax.dynamic_slice_in_dim(along_z, core * z_low, z_low, axis=0)
    theirs = lax.dynamic_slice_in_dim(along_z, (1 - core) * z_low, z_low, axis=0)
    both = jnp.stack([mine, swap_cores(theirs)]).reshape(count, lanes)

    first_table, _, first_rows = row_tables(SECTIONS[:1], 1, z_low, cores)
    rest_table, _, _ = row_tables(SECTIONS[1:], toks, z_low, cores)
    rest = lax.dynamic_index_in_dim(jnp.asarray(rest_table), tok, axis=1, keepdims=False)
    rest = rest + jnp.asarray([[first_rows], [0], [0]], jnp.int32)
    rows, low, from_core = jnp.concatenate([jnp.asarray(first_table[:, 0]), rest], axis=1)
    order = ((from_core - core) % cores * z_low + low) * packed_rows + rows
    mover = order[:, None] == jnp.arange(count, dtype=jnp.int32)[None, :]
    ordered = f32_dot(mover.astype(jnp.bfloat16), both).astype(jnp.bfloat16)
    return ordered, first_table.shape[2]


def spread_weights(ordered, first_rows):
    left, right = near_on_ring(ordered, "x")
    far_first = pass_on(left[:first_rows], "x", 1)
    far_rest = pass_on(right[first_rows:], "x", -1)
    first = jnp.stack([ordered[:first_rows], left[:first_rows], far_first, right[:first_rows]])
    rest = jnp.stack([ordered[first_rows:], left[first_rows:], far_rest, right[first_rows:]])
    first_other = swap_cores(first)
    left, right = near_on_ring(rest, "tok")
    left, right, first_other = lax.optimization_barrier((left, right, first_other))
    far_low, far_high = ring_far(left, right, 0)
    along_y = jnp.stack([rest, left, jnp.concatenate([far_low, far_high], axis=0), right])
    return assemble(first[None], first_other[None], SECTIONS[:1], 1) + assemble(
        along_y, swap_cores(along_y), SECTIONS[1:], lax.axis_size("tok")
    )


def pass_on(value, axis, shift):
    return lax.ppermute(value, axis, cycle(lax.axis_size(axis), shift))


def near_on_ring(own, axis):
    return pass_on(own, axis, 1), pass_on(own, axis, -1)


def ring_far(left, right, axis):
    half = left.shape[axis] // 2
    low = lax.slice_in_dim(left, 0, half, axis=axis)
    high = lax.slice_in_dim(right, half, 2 * half, axis=axis)
    return pass_on(low, "tok", 1), pass_on(high, "tok", -1)


def assemble_kernel(places, at_ref, mine_ref, other_ref, *outs):
    toks, groups = mine_ref.shape[:2]
    tok, x, core = at_ref[0], at_ref[1], at_ref[2]
    for out, tiles in zip(outs, places):
        for tile, (place_tok, start, rows) in enumerate(tiles):
            tok_step = lax.rem(tok - place_tok + toks, toks) if toks > 1 else 0
            for x_step in range(groups):
                from_x = lax.rem(x - x_step + groups, groups)
                for source, half in ((mine_ref, core), (other_ref, 1 - core)):
                    out[from_x, half, :, tile * LANES : (tile + 1) * LANES] = source[
                        tok_step, x_step, start : start + rows, :
                    ]


def assemble(mine, other, sections, toks):
    groups = mine.shape[1]
    cores = lax.axis_size("c")
    _, places, _ = row_tables(sections, toks, lax.axis_size("z") // cores, cores)
    place = jnp.stack(
        [lax.axis_index("tok"), lax.axis_index("x"), lax.axis_index("c")]
    ).astype(jnp.int32)
    shapes = [
        jax.ShapeDtypeStruct((groups, cores, tiles[0][2], len(tiles) * LANES), jnp.bfloat16)
        for tiles in places
    ]
    full = pl.pallas_call(
        functools.partial(assemble_kernel, places),
        out_shape=shapes,
        in_specs=[pl.BlockSpec(memory_space=pltpu.SMEM)]
        + [pl.BlockSpec(memory_space=pltpu.VMEM)] * 2,
        out_specs=[pl.BlockSpec(memory_space=pltpu.VMEM)] * len(shapes),
        compiler_params=pltpu.CompilerParams(vmem_limit_bytes=VMEM_BYTES),
        cost_estimate=pl.CostEstimate(
            flops=0, bytes_accessed=4 * mine.size * 2, transcendentals=0
        ),
        name="assemble",
    )(place, mine, other)
    return [matrix.reshape(-1, matrix.shape[-1]) for matrix in full]


def embed_kernel(arrived_ref, matrix_ref, out_ref):
    groups, blocks, images, block_rows, part = arrived_ref.shape
    for image in range(images):
        total = None
        for group in range(groups):
            rows = arrived_ref[group, :, image].astype(jnp.float32)
            rows = rows.reshape(blocks * block_rows, part).astype(jnp.bfloat16)
            product = f32_dot(rows, matrix_ref[group * part : (group + 1) * part, :])
            total = product if total is None else total + product
        out_ref[image] = total.astype(jnp.bfloat16)


def embed(arrived, matrix):
    groups, blocks, images, block_rows, part = arrived.shape
    rows, width = blocks * block_rows, matrix.shape[1]
    return pl.pallas_call(
        embed_kernel,
        out_shape=jax.ShapeDtypeStruct((images, rows, width), jnp.bfloat16),
        compiler_params=pltpu.CompilerParams(vmem_limit_bytes=VMEM_BYTES),
        cost_estimate=pl.CostEstimate(
            flops=2 * images * rows * matrix.size,
            bytes_accessed=2 * (arrived.size + matrix.size + images * rows * width),
            transcendentals=0,
        ),
        name="embed",
    )(arrived, matrix)


def head_halves():
    return lax.broadcasted_iota(jnp.int32, (1, LANES), 1) < HD


def fold(queries, key_ref, value_ref, first_key, first_value, totals, chunk=256):
    others = key_ref.shape[0]
    low_half = head_halves()
    across = (((1,), (1,)), ((), ()))
    done = []
    for pair in range(HEADS // 2):
        query = queries[:, pair * LANES : (pair + 1) * LANES]
        blank = jnp.zeros_like(query)
        low_query = jnp.where(low_half, query, blank)
        high_query = jnp.where(low_half, blank, query)
        low_total, high_total = totals[2 * pair], totals[2 * pair + 1]
        for start in range(0, others, chunk):
            at = slice(start, start + chunk)
            keys = key_ref[at, first_key + pair * LANES : first_key + (pair + 1) * LANES]
            values = value_ref[at, first_value + pair * LANES : first_value + (pair + 1) * LANES]
            ones = jnp.ones_like(values)
            scores = lax.dot_general(low_query, keys, across, preferred_element_type=jnp.float32)
            weights = jnp.exp(scores).astype(jnp.bfloat16)
            low_total = low_total + f32_dot(weights, jnp.where(low_half, values, ones))
            scores = lax.dot_general(high_query, keys, across, preferred_element_type=jnp.float32)
            weights = jnp.exp(scores).astype(jnp.bfloat16)
            high_total = high_total + f32_dot(weights, jnp.where(low_half, ones, values))
        done += [low_total, high_total]
    return done


def finish(totals):
    low_half = head_halves()
    done = []
    for pair in range(HEADS // 2):
        low_total, high_total = totals[2 * pair], totals[2 * pair + 1]
        numer = jnp.where(low_half, low_total, high_total)
        denom = pltpu.roll(jnp.where(low_half, high_total, low_total), HD, 1)
        done.append((numer / denom).astype(jnp.bfloat16))
    return jnp.concatenate(done, axis=1)


def nothing(rows):
    return [jnp.zeros((rows, LANES), jnp.float32)] * HEADS


def scaled(queries):
    return (queries.astype(jnp.bfloat16).astype(jnp.float32) * HD**-0.5).astype(jnp.bfloat16)


def self_kernel(first, last, pieces, *refs):
    refs = list(refs)
    piece_refs = [refs.pop(0) for _ in range(pieces)]
    if not first:
        query_ref, totals_in = refs.pop(0), refs.pop(0)
    if last:
        own_ref = refs.pop(0)
    project_ref, keyval_ref = refs.pop(0), refs.pop(0)
    width = keyval_ref.shape[1] // 2
    if last:
        output_ref, second_ref = refs.pop(0), refs.pop(0)
    cross_ref = refs.pop(0)
    if first:
        query_out = refs.pop(0)
    if last:
        after_ref, next_ref = refs.pop(0), refs.pop(0)
    else:
        totals_out = refs.pop(0)
    scratch = refs.pop(0)
    at = 0
    for ref in piece_refs:
        normed = normalize(ref[0].astype(jnp.float32)).astype(jnp.bfloat16)
        here = slice(at, at + normed.shape[0])
        scratch[here] = f32_dot(normed, project_ref[:, width:]).astype(jnp.bfloat16)
        cross_ref[0, here] = f32_dot(normed, keyval_ref[...]).astype(jnp.bfloat16)
        at += normed.shape[0]
    if first:
        queries = scaled(f32_dot(normed, project_ref[:, :width]))
        query_out[0] = queries
        totals = nothing(queries.shape[0])
    else:
        queries = query_ref[0]
        totals = [totals_in[0, head] for head in range(HEADS)]
    totals = fold(queries, scratch, scratch, 0, width, totals)
    if last:
        after = own_ref[0].astype(jnp.float32) + f32_dot(finish(totals), output_ref[...])
        after_ref[0] = after
        second = normalize(after).astype(jnp.bfloat16)
        next_ref[0] = scaled(f32_dot(second, second_ref[...]))
    else:
        for head in range(HEADS):
            totals_out[0, head] = totals[head]


def per_image(shape):
    return pl.BlockSpec((1,) + shape[1:], lambda i: (i,) + (0,) * (len(shape) - 1))


def whole(matrix):
    return pl.BlockSpec(matrix.shape, lambda i: (0, 0))


def self_step(pieces, project, keyval, carry=None, ending=None):
    first, last = carry is None, ending is not None
    images, _, model = pieces[0].shape
    width = keyval.shape[1] // 2
    others = sum(piece.shape[1] for piece in pieces)
    arrays = list(pieces) + list(carry or ())
    matrices = [project, keyval]
    if last:
        arrays.append(ending[0])
        matrices += ending[1:]
    rows = pieces[0].shape[1] if first else carry[0].shape[1]
    shapes = [jax.ShapeDtypeStruct((images, others, 2 * width), jnp.bfloat16)]
    if first:
        shapes.append(jax.ShapeDtypeStruct((images, rows, width), jnp.bfloat16))
    if last:
        shapes.append(jax.ShapeDtypeStruct((images, rows, model), jnp.float32))
        shapes.append(jax.ShapeDtypeStruct((images, rows, width), jnp.bfloat16))
    else:
        shapes.append(jax.ShapeDtypeStruct((images, HEADS, rows, LANES), jnp.float32))
    return pl.pallas_call(
        functools.partial(self_kernel, first, last, len(pieces)),
        grid=(images,),
        out_shape=shapes,
        in_specs=[per_image(array.shape) for array in arrays] + [whole(matrix) for matrix in matrices],
        out_specs=[per_image(shape.shape) for shape in shapes],
        scratch_shapes=[pltpu.VMEM((others, 2 * width), jnp.bfloat16)],
        compiler_params=pltpu.CompilerParams(vmem_limit_bytes=VMEM_BYTES),
        cost_estimate=pl.CostEstimate(
            flops=2 * images * (others * model * 4 * width + 4 * rows * others * width),
            bytes_accessed=2 * sum(matrix.size for matrix in matrices)
            + sum(array.size * array.dtype.itemsize for array in arrays),
            transcendentals=images * HEADS * rows * others,
        ),
        name="self_step",
    )(*arrays, *matrices)


def cross_kernel(pieces, after_ref, query_ref, *refs):
    keyval_refs, output_ref, out_ref = refs[:pieces], refs[pieces], refs[pieces + 1]
    width = output_ref.shape[0]
    halves, blocks, block_rows, part = out_ref.shape[1:]
    queries = query_ref[0]
    totals = nothing(queries.shape[0])
    for ref in keyval_refs:
        keyval = ref.at[0]
        totals = fold(queries, keyval, keyval, 0, width, totals)
    mixed = after_ref[0] + f32_dot(finish(totals), output_ref[...])
    for half in range(halves):
        columns = mixed[:, half * part : (half + 1) * part]
        out_ref[0, half] = columns.reshape(blocks, block_rows, part).astype(jnp.bfloat16)


def cross_block(after, query, keyvals, output, halves, block_rows):
    images, rows, model = after.shape
    width = output.shape[0]
    everyone = sum(keyval.shape[1] for keyval in keyvals)
    shape = (images, halves, rows // block_rows, block_rows, model // halves)
    return pl.pallas_call(
        functools.partial(cross_kernel, len(keyvals)),
        grid=(images,),
        out_shape=jax.ShapeDtypeStruct(shape, jnp.bfloat16),
        in_specs=[per_image(after.shape), per_image(query.shape)]
        + [
            pl.BlockSpec((1,) + keyval.shape[1:], lambda i: (images - 1 - i, 0, 0))
            for keyval in keyvals
        ]
        + [whole(output)],
        out_specs=per_image(shape),
        compiler_params=pltpu.CompilerParams(vmem_limit_bytes=VMEM_BYTES),
        cost_estimate=pl.CostEstimate(
            flops=2 * images * (4 * rows * everyone * width + rows * model * width),
            bytes_accessed=4 * after.size + 2 * (query.size + output.size + after.size),
            transcendentals=images * HEADS * rows * everyone,
        ),
        name="cross_block",
    )(after, query, *keyvals, output)


def shards(tokens, pair_list, owner_base, *weight_shards):
    groups = lax.axis_size("x")
    row_devices = lax.axis_size("z") * lax.axis_size("c")
    devices = groups * row_devices
    column = lax.axis_index("z") * lax.axis_size("c") + lax.axis_index("c")
    spread, block_rows, encoder = tokens.shape[1], tokens.shape[3], tokens.shape[4]
    held = tokens.reshape(spread, block_rows, encoder)
    part = encoder // groups

    x = lax.axis_index("x")
    parted = jnp.stack([held[:, :, i * part : (i + 1) * part] for i in range(groups)])
    parted, weight_shards = lax.optimization_barrier((parted, weight_shards))
    along_z = start_weights(weight_shards)
    pieces = []
    for step in range(groups):
        piece = lax.dynamic_index_in_dim(parted, (x + step) % groups, axis=0, keepdims=False)
        pieces.append(piece if step == 0 else pass_on(piece, "x", step))
    pieces = jnp.concatenate(pieces, axis=0)

    bases = owner_base[pair_list]
    slot = (column - bases) % spread
    source = ((bases + slot - column) // row_devices) % groups
    place = source * spread + slot
    held_at = (x - source) % groups * spread + slot
    outgoing = jnp.take(pieces, held_at.reshape(-1), axis=0, mode="clip").reshape(
        devices, 2, block_rows, part
    )
    outgoing, along_z = lax.optimization_barrier((outgoing, along_z))
    arrived = lax.all_to_all(outgoing, IMG, 0, 0, tiled=True)
    arrived = arrived.reshape(groups, row_devices, 2, block_rows, part)
    full = spread_weights(*order_weights(along_z))
    embed_full, project_full, self_out_full, query_full, keyval_full, cross_out_full = full
    model_width = embed_full.shape[1]

    embedded = embed(arrived, embed_full)
    left, right = near_on_ring(embedded, "tok")
    far_low, far_high = ring_far(left, right, 1)
    near_keyval, queries, totals = self_step([left, right, embedded], project_full, keyval_full)
    far_keyval, after_self, cross_queries = self_step(
        [far_low, far_high], project_full, keyval_full, (queries, totals),
        (embedded, self_out_full, query_full),
    )

    halves = groups // 2
    backward = cross_block(
        after_self, cross_queries, [near_keyval, far_keyval], cross_out_full,
        halves, block_rows,
    ).reshape(devices, block_rows, model_width // halves)
    returned = lax.all_to_all(backward, IMG, 0, 0, tiled=True)
    my_half = x // halves
    my_place = lax.dynamic_index_in_dim(place, my_half, axis=1, keepdims=False)
    selector = (
        my_place[None, :] == jnp.arange(devices, dtype=jnp.int32)[:, None]
    ).astype(jnp.bfloat16)
    partial = jnp.einsum(
        "ge,ebd->gbd", selector, returned, preferred_element_type=jnp.float32
    ).astype(jnp.bfloat16)
    home = lax.all_to_all(
        partial.reshape(groups, spread, block_rows, model_width // halves), "x", 0, 0, tiled=True
    )
    home = home.reshape(2, halves, spread, block_rows, model_width // halves)
    total = home[0].astype(jnp.float32) + home[1].astype(jnp.float32)
    summed = jnp.concatenate([total[half] for half in range(halves)], axis=-1)
    return summed.astype(jnp.bfloat16).reshape(1, spread, 1, block_rows, model_width)


def solution(mesh):
    chips = Mesh(mesh.devices.reshape(4, 16, 2, 4), ("x", "z", "c", "tok"))
    rows = P(IMG, None)
    tokens = P(IMG, None, "tok", None, None)
    return jax.shard_map(
        shards,
        mesh=chips,
        in_specs=(tokens, P(), P()) + (rows,) * 6,
        out_specs=tokens,
        check_vma=False,
    )
```

```python
import functools

import jax
import jax.numpy as jnp
import numpy as np
from jax import lax
from jax.experimental import pallas as pl
from jax.experimental.pallas import tpu as pltpu
from jax.sharding import Mesh, PartitionSpec as P

HEADS = 6
HD = 64
LANES = 128
IMG = ("x", "z", "c")
VMEM_BYTES = 50 * 1024 * 1024

SECTIONS = (
    ("embed", 8, 6),
    ("project", 6, 9),
    ("self_out", 3, 6),
    ("query", 6, 3),
    ("keyval", 6, 6),
    ("cross_out", 3, 6),
)
def f32_dot(left, right):
    return jnp.dot(left, right, preferred_element_type=jnp.float32)


def normalize(values):
    mean_value = jnp.mean(values, axis=-1, keepdims=True)
    centred = values - mean_value
    variance = jnp.mean(centred * centred, axis=-1, keepdims=True)
    return centred * lax.rsqrt(variance + 1e-06)


def row_tables(sections, toks, z_low, cores):
    total = sum(rows * tiles for _, rows, tiles in sections)
    quarter = total // toks
    table = np.zeros((3, toks, quarter * z_low * cores), np.int32)
    places = []
    at = 0
    for _, rows, tiles in sections:
        places.append([])
        for _ in range(tiles):
            tok, start = divmod(at, quarter)
            assert start + rows <= quarter
            out = start * z_low * cores
            places[-1].append((tok, out, rows * z_low * cores))
            for z in range(z_low):
                for core in range(cores):
                    for row in range(rows):
                        table[:, tok, out] = (start + row, z, core)
                        out += 1
            at += rows
    return table, places, quarter


def pack_kernel(toks, tok_ref, *refs):
    shard_refs, out_ref = refs[:-1], refs[-1]
    tiles = [
        [(ref, slice(tile * LANES, (tile + 1) * LANES)) for tile in range(count)]
        for ref, (_, _, count) in zip(shard_refs, SECTIONS)
    ]
    rest = sum(tiles[1:], [])
    quarter = sum(ref.shape[0] for ref, _ in rest) // toks
    groups = [list(tiles[0]) for _ in range(toks)]
    at = 0
    for ref, columns in rest:
        groups[at // quarter].append((ref, columns))
        at += ref.shape[0]
    for tok in range(toks):
        @pl.when(tok_ref[0] == tok)
        def _(tok=tok):
            values = [ref[:, columns].astype(jnp.float32) for ref, columns in groups[tok]]
            out_ref[...] = jnp.concatenate(values, axis=0).astype(jnp.bfloat16)


def pack(shards_in):
    toks = lax.axis_size("tok")
    sizes = [rows * tiles for _, rows, tiles in SECTIONS]
    return pl.pallas_call(
        functools.partial(pack_kernel, toks),
        out_shape=jax.ShapeDtypeStruct((sizes[0] + sum(sizes[1:]) // toks, LANES), jnp.bfloat16),
        in_specs=[pl.BlockSpec(memory_space=pltpu.SMEM)]
        + [pl.BlockSpec(memory_space=pltpu.VMEM)] * len(shards_in),
        out_specs=pl.BlockSpec(memory_space=pltpu.VMEM),
        name="pack",
    )(lax.axis_index("tok").astype(jnp.int32)[None], *shards_in)


def cycle(count, shift):
    return [(i, (i + shift) % count) for i in range(count)]


def swap_cores(value):
    return lax.ppermute(value, "c", cycle(lax.axis_size("c"), 1))


def start_weights(shards_in):
    packed = pack(shards_in)
    copies = jnp.broadcast_to(packed[None], (lax.axis_size("z"),) + packed.shape)
    return lax.all_to_all(copies, "z", 0, 0, tiled=True)


def order_weights(along_z):
    toks, cores, depth = lax.axis_size("tok"), lax.axis_size("c"), lax.axis_size("z")
    tok, core = lax.axis_index("tok"), lax.axis_index("c")
    _, packed_rows, lanes = along_z.shape
    z_low = depth // cores
    count = cores * z_low * packed_rows
    mine = lax.dynamic_slice_in_dim(along_z, core * z_low, z_low, axis=0)
    theirs = lax.dynamic_slice_in_dim(along_z, (1 - core) * z_low, z_low, axis=0)
    both = jnp.stack([mine, swap_cores(theirs)]).reshape(count, lanes)

    first_table, _, first_rows = row_tables(SECTIONS[:1], 1, z_low, cores)
    rest_table, _, _ = row_tables(SECTIONS[1:], toks, z_low, cores)
    rest = lax.dynamic_index_in_dim(jnp.asarray(rest_table), tok, axis=1, keepdims=False)
    rest = rest + jnp.asarray([[first_rows], [0], [0]], jnp.int32)
    rows, low, from_core = jnp.concatenate([jnp.asarray(first_table[:, 0]), rest], axis=1)
    order = ((from_core - core) % cores * z_low + low) * packed_rows + rows
    mover = order[:, None] == jnp.arange(count, dtype=jnp.int32)[None, :]
    ordered = f32_dot(mover.astype(jnp.bfloat16), both).astype(jnp.bfloat16)
    return ordered, first_table.shape[2]


def spread_weights(ordered, first_rows):
    left, right = near_on_ring(ordered, "x")
    far_first = pass_on(left[:first_rows], "x", 1)
    far_rest = pass_on(right[first_rows:], "x", -1)
    first = jnp.stack([ordered[:first_rows], left[:first_rows], far_first, right[:first_rows]])
    rest = jnp.stack([ordered[first_rows:], left[first_rows:], far_rest, right[first_rows:]])
    return assemble(first[None], swap_cores(first)[None], SECTIONS[:1], 1)[0], rest


def finish_weights(rest, left, right):
    far_low, far_high = ring_far(left, right, 0)
    along_y = jnp.stack([rest, left, jnp.concatenate([far_low, far_high], axis=0), right])
    return assemble(along_y, swap_cores(along_y), SECTIONS[1:], lax.axis_size("tok"))


def pass_on(value, axis, shift):
    return lax.ppermute(value, axis, cycle(lax.axis_size(axis), shift))


def near_on_ring(own, axis):
    return pass_on(own, axis, 1), pass_on(own, axis, -1)


def ring_far(left, right, axis):
    half = left.shape[axis] // 2
    low = lax.slice_in_dim(left, 0, half, axis=axis)
    high = lax.slice_in_dim(right, half, 2 * half, axis=axis)
    return pass_on(low, "tok", 1), pass_on(high, "tok", -1)


def assemble_kernel(places, at_ref, mine_ref, other_ref, *outs):
    toks, groups = mine_ref.shape[:2]
    tok, x, core = at_ref[0], at_ref[1], at_ref[2]
    for out, tiles in zip(outs, places):
        for tile, (place_tok, start, rows) in enumerate(tiles):
            tok_step = lax.rem(tok - place_tok + toks, toks) if toks > 1 else 0
            for x_step in range(groups):
                from_x = lax.rem(x - x_step + groups, groups)
                for source, half in ((mine_ref, core), (other_ref, 1 - core)):
                    out[from_x, half, :, tile * LANES : (tile + 1) * LANES] = source[
                        tok_step, x_step, start : start + rows, :
                    ]


def assemble(mine, other, sections, toks):
    groups = mine.shape[1]
    cores = lax.axis_size("c")
    _, places, _ = row_tables(sections, toks, lax.axis_size("z") // cores, cores)
    place = jnp.stack(
        [lax.axis_index("tok"), lax.axis_index("x"), lax.axis_index("c")]
    ).astype(jnp.int32)
    shapes = [
        jax.ShapeDtypeStruct((groups, cores, tiles[0][2], len(tiles) * LANES), jnp.bfloat16)
        for tiles in places
    ]
    full = pl.pallas_call(
        functools.partial(assemble_kernel, places),
        out_shape=shapes,
        in_specs=[pl.BlockSpec(memory_space=pltpu.SMEM)]
        + [pl.BlockSpec(memory_space=pltpu.VMEM)] * 2,
        out_specs=[pl.BlockSpec(memory_space=pltpu.VMEM)] * len(shapes),
        compiler_params=pltpu.CompilerParams(vmem_limit_bytes=VMEM_BYTES),
        cost_estimate=pl.CostEstimate(
            flops=0, bytes_accessed=4 * mine.size * 2, transcendentals=0
        ),
        name="assemble",
    )(place, mine, other)
    return [matrix.reshape(-1, matrix.shape[-1]) for matrix in full]


def embed_kernel(arrived_ref, matrix_ref, out_ref):
    groups, blocks, images, block_rows, part = arrived_ref.shape
    for image in range(images):
        total = None
        for group in range(groups):
            rows = arrived_ref[group, :, image].astype(jnp.float32)
            rows = rows.reshape(blocks * block_rows, part).astype(jnp.bfloat16)
            product = f32_dot(rows, matrix_ref[group * part : (group + 1) * part, :])
            total = product if total is None else total + product
        out_ref[image] = total.astype(jnp.bfloat16)


def embed(arrived, matrix):
    groups, blocks, images, block_rows, part = arrived.shape
    rows, width = blocks * block_rows, matrix.shape[1]
    return pl.pallas_call(
        embed_kernel,
        out_shape=jax.ShapeDtypeStruct((images, rows, width), jnp.bfloat16),
        compiler_params=pltpu.CompilerParams(vmem_limit_bytes=VMEM_BYTES),
        cost_estimate=pl.CostEstimate(
            flops=2 * images * rows * matrix.size,
            bytes_accessed=2 * (arrived.size + matrix.size + images * rows * width),
            transcendentals=0,
        ),
        name="embed",
    )(arrived, matrix)


def head_halves():
    return lax.broadcasted_iota(jnp.int32, (1, LANES), 1) < HD


def fold(queries, key_ref, value_ref, first_key, first_value, totals, chunk=256):
    others = key_ref.shape[0]
    low_half = head_halves()
    across = (((1,), (1,)), ((), ()))
    done = []
    for pair in range(HEADS // 2):
        query = queries[:, pair * LANES : (pair + 1) * LANES]
        blank = jnp.zeros_like(query)
        low_query = jnp.where(low_half, query, blank)
        high_query = jnp.where(low_half, blank, query)
        low_total, high_total = totals[2 * pair], totals[2 * pair + 1]
        for start in range(0, others, chunk):
            at = slice(start, start + chunk)
            keys = key_ref[at, first_key + pair * LANES : first_key + (pair + 1) * LANES]
            values = value_ref[at, first_value + pair * LANES : first_value + (pair + 1) * LANES]
            ones = jnp.ones_like(values)
            scores = lax.dot_general(low_query, keys, across, preferred_element_type=jnp.float32)
            weights = jnp.exp(scores).astype(jnp.bfloat16)
            low_total = low_total + f32_dot(weights, jnp.where(low_half, values, ones))
            scores = lax.dot_general(high_query, keys, across, preferred_element_type=jnp.float32)
            weights = jnp.exp(scores).astype(jnp.bfloat16)
            high_total = high_total + f32_dot(weights, jnp.where(low_half, ones, values))
        done += [low_total, high_total]
    return done


def finish(totals):
    low_half = head_halves()
    done = []
    for pair in range(HEADS // 2):
        low_total, high_total = totals[2 * pair], totals[2 * pair + 1]
        numer = jnp.where(low_half, low_total, high_total)
        denom = pltpu.roll(jnp.where(low_half, high_total, low_total), HD, 1)
        done.append((numer / denom).astype(jnp.bfloat16))
    return jnp.concatenate(done, axis=1)


def nothing(rows):
    return [jnp.zeros((rows, LANES), jnp.float32)] * HEADS


def scaled(queries):
    return (queries.astype(jnp.bfloat16).astype(jnp.float32) * HD**-0.5).astype(jnp.bfloat16)


def self_kernel(first, last, pieces, *refs):
    refs = list(refs)
    piece_refs = [refs.pop(0) for _ in range(pieces)]
    if not first:
        query_ref, totals_in = refs.pop(0), refs.pop(0)
    if last:
        own_ref = refs.pop(0)
    project_ref, keyval_ref = refs.pop(0), refs.pop(0)
    width = keyval_ref.shape[1] // 2
    if last:
        output_ref, second_ref = refs.pop(0), refs.pop(0)
    cross_ref = refs.pop(0)
    if first:
        query_out = refs.pop(0)
    if last:
        after_ref, next_ref = refs.pop(0), refs.pop(0)
    else:
        totals_out = refs.pop(0)
    scratch = refs.pop(0)
    at = 0
    for ref in piece_refs:
        normed = normalize(ref[0].astype(jnp.float32)).astype(jnp.bfloat16)
        here = slice(at, at + normed.shape[0])
        scratch[here] = f32_dot(normed, project_ref[:, width:]).astype(jnp.bfloat16)
        cross_ref[0, here] = f32_dot(normed, keyval_ref[...]).astype(jnp.bfloat16)
        at += normed.shape[0]
    if first:
        queries = scaled(f32_dot(normed, project_ref[:, :width]))
        query_out[0] = queries
        totals = nothing(queries.shape[0])
    else:
        queries = query_ref[0]
        totals = [totals_in[0, head] for head in range(HEADS)]
    totals = fold(queries, scratch, scratch, 0, width, totals)
    if last:
        after = own_ref[0].astype(jnp.float32) + f32_dot(finish(totals), output_ref[...])
        after_ref[0] = after
        second = normalize(after).astype(jnp.bfloat16)
        next_ref[0] = scaled(f32_dot(second, second_ref[...]))
    else:
        for head in range(HEADS):
            totals_out[0, head] = totals[head]


def per_image(shape):
    return pl.BlockSpec((1,) + shape[1:], lambda i: (i,) + (0,) * (len(shape) - 1))


def whole(matrix):
    return pl.BlockSpec(matrix.shape, lambda i: (0, 0))


def self_step(pieces, project, keyval, carry=None, ending=None):
    first, last = carry is None, ending is not None
    images, _, model = pieces[0].shape
    width = keyval.shape[1] // 2
    others = sum(piece.shape[1] for piece in pieces)
    arrays = list(pieces) + list(carry or ())
    matrices = [project, keyval]
    if last:
        arrays.append(ending[0])
        matrices += ending[1:]
    rows = pieces[0].shape[1] if first else carry[0].shape[1]
    shapes = [jax.ShapeDtypeStruct((images, others, 2 * width), jnp.bfloat16)]
    if first:
        shapes.append(jax.ShapeDtypeStruct((images, rows, width), jnp.bfloat16))
    if last:
        shapes.append(jax.ShapeDtypeStruct((images, rows, model), jnp.float32))
        shapes.append(jax.ShapeDtypeStruct((images, rows, width), jnp.bfloat16))
    else:
        shapes.append(jax.ShapeDtypeStruct((images, HEADS, rows, LANES), jnp.float32))
    return pl.pallas_call(
        functools.partial(self_kernel, first, last, len(pieces)),
        grid=(images,),
        out_shape=shapes,
        in_specs=[per_image(array.shape) for array in arrays] + [whole(matrix) for matrix in matrices],
        out_specs=[per_image(shape.shape) for shape in shapes],
        scratch_shapes=[pltpu.VMEM((others, 2 * width), jnp.bfloat16)],
        compiler_params=pltpu.CompilerParams(vmem_limit_bytes=VMEM_BYTES),
        cost_estimate=pl.CostEstimate(
            flops=2 * images * (others * model * 4 * width + 4 * rows * others * width),
            bytes_accessed=2 * sum(matrix.size for matrix in matrices)
            + sum(array.size * array.dtype.itemsize for array in arrays),
            transcendentals=images * HEADS * rows * others,
        ),
        name="self_step",
    )(*arrays, *matrices)


def cross_kernel(pieces, after_ref, query_ref, *refs):
    keyval_refs, output_ref, out_ref = refs[:pieces], refs[pieces], refs[pieces + 1]
    width = output_ref.shape[0]
    halves, blocks, block_rows, part = out_ref.shape[1:]
    queries = query_ref[0]
    totals = nothing(queries.shape[0])
    for ref in keyval_refs:
        keyval = ref.at[0]
        totals = fold(queries, keyval, keyval, 0, width, totals)
    mixed = after_ref[0] + f32_dot(finish(totals), output_ref[...])
    for half in range(halves):
        columns = mixed[:, half * part : (half + 1) * part]
        out_ref[0, half] = columns.reshape(blocks, block_rows, part).astype(jnp.bfloat16)


def cross_block(after, query, keyvals, output, halves, block_rows):
    images, rows, model = after.shape
    width = output.shape[0]
    everyone = sum(keyval.shape[1] for keyval in keyvals)
    shape = (images, halves, rows // block_rows, block_rows, model // halves)
    return pl.pallas_call(
        functools.partial(cross_kernel, len(keyvals)),
        grid=(images,),
        out_shape=jax.ShapeDtypeStruct(shape, jnp.bfloat16),
        in_specs=[per_image(after.shape), per_image(query.shape)]
        + [
            pl.BlockSpec((1,) + keyval.shape[1:], lambda i: (images - 1 - i, 0, 0))
            for keyval in keyvals
        ]
        + [whole(output)],
        out_specs=per_image(shape),
        compiler_params=pltpu.CompilerParams(vmem_limit_bytes=VMEM_BYTES),
        cost_estimate=pl.CostEstimate(
            flops=2 * images * (4 * rows * everyone * width + rows * model * width),
            bytes_accessed=4 * after.size + 2 * (query.size + output.size + after.size),
            transcendentals=images * HEADS * rows * everyone,
        ),
        name="cross_block",
    )(after, query, *keyvals, output)


def shards(tokens, pair_list, owner_base, *weight_shards):
    groups = lax.axis_size("x")
    row_devices = lax.axis_size("z") * lax.axis_size("c")
    devices = groups * row_devices
    column = lax.axis_index("z") * lax.axis_size("c") + lax.axis_index("c")
    spread, block_rows, encoder = tokens.shape[1], tokens.shape[3], tokens.shape[4]
    held = tokens.reshape(spread, block_rows, encoder)
    part = encoder // groups

    x = lax.axis_index("x")
    parted = jnp.stack([held[:, :, i * part : (i + 1) * part] for i in range(groups)])
    parted, weight_shards = lax.optimization_barrier((parted, weight_shards))
    along_z = start_weights(weight_shards)
    pieces = []
    for step in range(groups):
        piece = lax.dynamic_index_in_dim(parted, (x + step) % groups, axis=0, keepdims=False)
        pieces.append(piece if step == 0 else pass_on(piece, "x", step))
    pieces = jnp.concatenate(pieces, axis=0)

    bases = owner_base[pair_list]
    slot = (column - bases) % spread
    source = ((bases + slot - column) // row_devices) % groups
    place = source * spread + slot
    held_at = (x - source) % groups * spread + slot
    outgoing = jnp.take(pieces, held_at.reshape(-1), axis=0, mode="clip").reshape(
        devices, 2, block_rows, part
    )
    outgoing, along_z = lax.optimization_barrier((outgoing, along_z))
    arrived = lax.all_to_all(outgoing, IMG, 0, 0, tiled=True)
    arrived = arrived.reshape(groups, row_devices, 2, block_rows, part)
    embed_full, rest = spread_weights(*order_weights(along_z))
    model_width = embed_full.shape[1]
    rest_left, rest_right = near_on_ring(rest, "tok")
    embedded = embed(arrived, embed_full)
    rest_left, rest_right, embedded = lax.optimization_barrier((rest_left, rest_right, embedded))
    project_full, self_out_full, query_full, keyval_full, cross_out_full = finish_weights(
        rest, rest_left, rest_right
    )

    left, right = near_on_ring(embedded, "tok")
    far_low, far_high = ring_far(left, right, 1)
    near_keyval, queries, totals = self_step([left, right, embedded], project_full, keyval_full)
    far_keyval, after_self, cross_queries = self_step(
        [far_low, far_high], project_full, keyval_full, (queries, totals),
        (embedded, self_out_full, query_full),
    )

    halves = groups // 2
    backward = cross_block(
        after_self, cross_queries, [near_keyval, far_keyval], cross_out_full,
        halves, block_rows,
    ).reshape(devices, block_rows, model_width // halves)
    returned = lax.all_to_all(backward, IMG, 0, 0, tiled=True)
    my_half = x // halves
    my_place = lax.dynamic_index_in_dim(place, my_half, axis=1, keepdims=False)
    selector = (
        my_place[None, :] == jnp.arange(devices, dtype=jnp.int32)[:, None]
    ).astype(jnp.bfloat16)
    partial = jnp.einsum(
        "ge,ebd->gbd", selector, returned, preferred_element_type=jnp.float32
    ).astype(jnp.bfloat16)
    home = lax.all_to_all(
        partial.reshape(groups, spread, block_rows, model_width // halves), "x", 0, 0, tiled=True
    )
    home = home.reshape(2, halves, spread, block_rows, model_width // halves)
    total = home[0].astype(jnp.float32) + home[1].astype(jnp.float32)
    summed = jnp.concatenate([total[half] for half in range(halves)], axis=-1)
    return summed.astype(jnp.bfloat16).reshape(1, spread, 1, block_rows, model_width)


def solution(mesh):
    chips = Mesh(mesh.devices.reshape(4, 16, 2, 4), ("x", "z", "c", "tok"))
    rows = P(IMG, None)
    tokens = P(IMG, None, "tok", None, None)
    return jax.shard_map(
        shards,
        mesh=chips,
        in_specs=(tokens, P(), P()) + (rows,) * 6,
        out_specs=tokens,
        check_vma=False,
    )
```

```python
import functools

import jax
import jax.numpy as jnp
import numpy as np
from jax import lax
from jax.experimental import pallas as pl
from jax.experimental.pallas import tpu as pltpu
from jax.sharding import Mesh, PartitionSpec as P

HEADS = 6
HD = 64
LANES = 128
IMG = ("x", "z", "c")
VMEM_BYTES = 50 * 1024 * 1024

SECTIONS = (
    ("embed", 8, 6),
    ("project", 6, 9),
    ("self_out", 3, 6),
    ("query", 6, 3),
    ("keyval", 6, 6),
    ("cross_out", 3, 6),
)
def f32_dot(left, right):
    return jnp.dot(left, right, preferred_element_type=jnp.float32)


def normalize(values):
    mean_value = jnp.mean(values, axis=-1, keepdims=True)
    centred = values - mean_value
    variance = jnp.mean(centred * centred, axis=-1, keepdims=True)
    return centred * lax.rsqrt(variance + 1e-06)


def row_tables(sections, toks, z_low, cores):
    total = sum(rows * tiles for _, rows, tiles in sections)
    quarter = total // toks
    table = np.zeros((3, toks, quarter * z_low * cores), np.int32)
    places = []
    at = 0
    for _, rows, tiles in sections:
        places.append([])
        for _ in range(tiles):
            tok, start = divmod(at, quarter)
            assert start + rows <= quarter
            out = start * z_low * cores
            places[-1].append((tok, out, rows * z_low * cores))
            for z in range(z_low):
                for core in range(cores):
                    for row in range(rows):
                        table[:, tok, out] = (start + row, z, core)
                        out += 1
            at += rows
    return table, places, quarter


def pack_kernel(toks, tok_ref, *refs):
    shard_refs, out_ref = refs[:-1], refs[-1]
    tiles = [
        [(ref, slice(tile * LANES, (tile + 1) * LANES)) for tile in range(count)]
        for ref, (_, _, count) in zip(shard_refs, SECTIONS)
    ]
    rest = sum(tiles[1:], [])
    quarter = sum(ref.shape[0] for ref, _ in rest) // toks
    groups = [list(tiles[0]) for _ in range(toks)]
    at = 0
    for ref, columns in rest:
        groups[at // quarter].append((ref, columns))
        at += ref.shape[0]
    for tok in range(toks):
        @pl.when(tok_ref[0] == tok)
        def _(tok=tok):
            values = [ref[:, columns].astype(jnp.float32) for ref, columns in groups[tok]]
            out_ref[...] = jnp.concatenate(values, axis=0).astype(jnp.bfloat16)


def pack(shards_in):
    toks = lax.axis_size("tok")
    sizes = [rows * tiles for _, rows, tiles in SECTIONS]
    return pl.pallas_call(
        functools.partial(pack_kernel, toks),
        out_shape=jax.ShapeDtypeStruct((sizes[0] + sum(sizes[1:]) // toks, LANES), jnp.bfloat16),
        in_specs=[pl.BlockSpec(memory_space=pltpu.SMEM)]
        + [pl.BlockSpec(memory_space=pltpu.VMEM)] * len(shards_in),
        out_specs=pl.BlockSpec(memory_space=pltpu.VMEM),
        name="pack",
    )(lax.axis_index("tok").astype(jnp.int32)[None], *shards_in)


def cycle(count, shift):
    return [(i, (i + shift) % count) for i in range(count)]


def swap_cores(value):
    return lax.ppermute(value, "c", cycle(lax.axis_size("c"), 1))


def start_weights(shards_in):
    packed = pack(shards_in)
    copies = jnp.broadcast_to(packed[None], (lax.axis_size("z"),) + packed.shape)
    return lax.all_to_all(copies, "z", 0, 0, tiled=True)


def order_weights(along_z):
    toks, cores, depth = lax.axis_size("tok"), lax.axis_size("c"), lax.axis_size("z")
    tok, core = lax.axis_index("tok"), lax.axis_index("c")
    _, packed_rows, lanes = along_z.shape
    z_low = depth // cores
    count = cores * z_low * packed_rows
    mine = lax.dynamic_slice_in_dim(along_z, core * z_low, z_low, axis=0)
    theirs = lax.dynamic_slice_in_dim(along_z, (1 - core) * z_low, z_low, axis=0)
    both = jnp.stack([mine, swap_cores(theirs)]).reshape(count, lanes)

    first_table, _, first_rows = row_tables(SECTIONS[:1], 1, z_low, cores)
    rest_table, _, _ = row_tables(SECTIONS[1:], toks, z_low, cores)
    rest = lax.dynamic_index_in_dim(jnp.asarray(rest_table), tok, axis=1, keepdims=False)
    rest = rest + jnp.asarray([[first_rows], [0], [0]], jnp.int32)
    rows, low, from_core = jnp.concatenate([jnp.asarray(first_table[:, 0]), rest], axis=1)
    order = ((from_core - core) % cores * z_low + low) * packed_rows + rows
    mover = order[:, None] == jnp.arange(count, dtype=jnp.int32)[None, :]
    ordered = f32_dot(mover.astype(jnp.bfloat16), both).astype(jnp.bfloat16)
    return ordered, first_table.shape[2]


def spread_weights(ordered, first_rows):
    left, right = near_on_ring(ordered, "x")
    far_first = pass_on(left[:first_rows], "x", 1)
    far_rest = pass_on(right[first_rows:], "x", -1)
    first = jnp.stack([ordered[:first_rows], left[:first_rows], far_first, right[:first_rows]])
    rest = jnp.stack([ordered[first_rows:], left[first_rows:], far_rest, right[first_rows:]])
    return assemble(first[None], swap_cores(first)[None], SECTIONS[:1], 1)[0], rest


def finish_weights(rest, left, right, before_swap):
    far_low, far_high = ring_far(left, right, 0)
    along_y = jnp.stack([rest, left, jnp.concatenate([far_low, far_high], axis=0), right])
    along_y, before_swap = lax.optimization_barrier((along_y, before_swap))
    return (
        assemble(along_y, swap_cores(along_y), SECTIONS[1:], lax.axis_size("tok")),
        before_swap,
    )


def pass_on(value, axis, shift):
    return lax.ppermute(value, axis, cycle(lax.axis_size(axis), shift))


def near_on_ring(own, axis):
    return pass_on(own, axis, 1), pass_on(own, axis, -1)


def ring_far(left, right, axis):
    half = left.shape[axis] // 2
    low = lax.slice_in_dim(left, 0, half, axis=axis)
    high = lax.slice_in_dim(right, half, 2 * half, axis=axis)
    return pass_on(low, "tok", 1), pass_on(high, "tok", -1)


def assemble_kernel(places, at_ref, mine_ref, other_ref, *outs):
    toks, groups = mine_ref.shape[:2]
    tok, x, core = at_ref[0], at_ref[1], at_ref[2]
    for out, tiles in zip(outs, places):
        for tile, (place_tok, start, rows) in enumerate(tiles):
            tok_step = lax.rem(tok - place_tok + toks, toks) if toks > 1 else 0
            for x_step in range(groups):
                from_x = lax.rem(x - x_step + groups, groups)
                for source, half in ((mine_ref, core), (other_ref, 1 - core)):
                    out[from_x, half, :, tile * LANES : (tile + 1) * LANES] = source[
                        tok_step, x_step, start : start + rows, :
                    ]


def assemble(mine, other, sections, toks):
    groups = mine.shape[1]
    cores = lax.axis_size("c")
    _, places, _ = row_tables(sections, toks, lax.axis_size("z") // cores, cores)
    place = jnp.stack(
        [lax.axis_index("tok"), lax.axis_index("x"), lax.axis_index("c")]
    ).astype(jnp.int32)
    shapes = [
        jax.ShapeDtypeStruct((groups, cores, tiles[0][2], len(tiles) * LANES), jnp.bfloat16)
        for tiles in places
    ]
    full = pl.pallas_call(
        functools.partial(assemble_kernel, places),
        out_shape=shapes,
        in_specs=[pl.BlockSpec(memory_space=pltpu.SMEM)]
        + [pl.BlockSpec(memory_space=pltpu.VMEM)] * 2,
        out_specs=[pl.BlockSpec(memory_space=pltpu.VMEM)] * len(shapes),
        compiler_params=pltpu.CompilerParams(vmem_limit_bytes=VMEM_BYTES),
        cost_estimate=pl.CostEstimate(
            flops=0, bytes_accessed=4 * mine.size * 2, transcendentals=0
        ),
        name="assemble",
    )(place, mine, other)
    return [matrix.reshape(-1, matrix.shape[-1]) for matrix in full]


def embed_kernel(arrived_ref, matrix_ref, out_ref):
    groups, blocks, images, block_rows, part = arrived_ref.shape
    for image in range(images):
        total = None
        for group in range(groups):
            rows = arrived_ref[group, :, image].astype(jnp.float32)
            rows = rows.reshape(blocks * block_rows, part).astype(jnp.bfloat16)
            product = f32_dot(rows, matrix_ref[group * part : (group + 1) * part, :])
            total = product if total is None else total + product
        out_ref[image] = total.astype(jnp.bfloat16)


def embed(arrived, matrix):
    groups, blocks, images, block_rows, part = arrived.shape
    rows, width = blocks * block_rows, matrix.shape[1]
    return pl.pallas_call(
        embed_kernel,
        out_shape=jax.ShapeDtypeStruct((images, rows, width), jnp.bfloat16),
        compiler_params=pltpu.CompilerParams(vmem_limit_bytes=VMEM_BYTES),
        cost_estimate=pl.CostEstimate(
            flops=2 * images * rows * matrix.size,
            bytes_accessed=2 * (arrived.size + matrix.size + images * rows * width),
            transcendentals=0,
        ),
        name="embed",
    )(arrived, matrix)


def head_halves():
    return lax.broadcasted_iota(jnp.int32, (1, LANES), 1) < HD


def fold(queries, key_ref, value_ref, first_key, first_value, totals, chunk=256):
    others = key_ref.shape[0]
    low_half = head_halves()
    across = (((1,), (1,)), ((), ()))
    done = []
    for pair in range(HEADS // 2):
        query = queries[:, pair * LANES : (pair + 1) * LANES]
        blank = jnp.zeros_like(query)
        low_query = jnp.where(low_half, query, blank)
        high_query = jnp.where(low_half, blank, query)
        low_total, high_total = totals[2 * pair], totals[2 * pair + 1]
        for start in range(0, others, chunk):
            at = slice(start, start + chunk)
            keys = key_ref[at, first_key + pair * LANES : first_key + (pair + 1) * LANES]
            values = value_ref[at, first_value + pair * LANES : first_value + (pair + 1) * LANES]
            ones = jnp.ones_like(values)
            scores = lax.dot_general(low_query, keys, across, preferred_element_type=jnp.float32)
            weights = jnp.exp(scores).astype(jnp.bfloat16)
            low_total = low_total + f32_dot(weights, jnp.where(low_half, values, ones))
            scores = lax.dot_general(high_query, keys, across, preferred_element_type=jnp.float32)
            weights = jnp.exp(scores).astype(jnp.bfloat16)
            high_total = high_total + f32_dot(weights, jnp.where(low_half, ones, values))
        done += [low_total, high_total]
    return done


def finish(totals):
    low_half = head_halves()
    done = []
    for pair in range(HEADS // 2):
        low_total, high_total = totals[2 * pair], totals[2 * pair + 1]
        numer = jnp.where(low_half, low_total, high_total)
        denom = pltpu.roll(jnp.where(low_half, high_total, low_total), HD, 1)
        done.append((numer / denom).astype(jnp.bfloat16))
    return jnp.concatenate(done, axis=1)


def nothing(rows):
    return [jnp.zeros((rows, LANES), jnp.float32)] * HEADS


def scaled(queries):
    return (queries.astype(jnp.bfloat16).astype(jnp.float32) * HD**-0.5).astype(jnp.bfloat16)


def self_kernel(first, last, pieces, *refs):
    refs = list(refs)
    piece_refs = [refs.pop(0) for _ in range(pieces)]
    if not first:
        query_ref, totals_in = refs.pop(0), refs.pop(0)
    if last:
        own_ref = refs.pop(0)
    project_ref, keyval_ref = refs.pop(0), refs.pop(0)
    width = keyval_ref.shape[1] // 2
    if last:
        output_ref, second_ref = refs.pop(0), refs.pop(0)
    cross_ref = refs.pop(0)
    if first:
        query_out = refs.pop(0)
    if last:
        after_ref, next_ref = refs.pop(0), refs.pop(0)
    else:
        totals_out = refs.pop(0)
    scratch = refs.pop(0)
    at = 0
    for ref in piece_refs:
        normed = normalize(ref[0].astype(jnp.float32)).astype(jnp.bfloat16)
        here = slice(at, at + normed.shape[0])
        scratch[here] = f32_dot(normed, project_ref[:, width:]).astype(jnp.bfloat16)
        cross_ref[0, here] = f32_dot(normed, keyval_ref[...]).astype(jnp.bfloat16)
        at += normed.shape[0]
    if first:
        queries = scaled(f32_dot(normed, project_ref[:, :width]))
        query_out[0] = queries
        totals = nothing(queries.shape[0])
    else:
        queries = query_ref[0]
        totals = [totals_in[0, head] for head in range(HEADS)]
    totals = fold(queries, scratch, scratch, 0, width, totals)
    if last:
        after = own_ref[0].astype(jnp.float32) + f32_dot(finish(totals), output_ref[...])
        after_ref[0] = after
        second = normalize(after).astype(jnp.bfloat16)
        next_ref[0] = scaled(f32_dot(second, second_ref[...]))
    else:
        for head in range(HEADS):
            totals_out[0, head] = totals[head]


def per_image(shape):
    return pl.BlockSpec((1,) + shape[1:], lambda i: (i,) + (0,) * (len(shape) - 1))


def whole(matrix):
    return pl.BlockSpec(matrix.shape, lambda i: (0, 0))


def self_step(pieces, project, keyval, carry=None, ending=None):
    first, last = carry is None, ending is not None
    images, _, model = pieces[0].shape
    width = keyval.shape[1] // 2
    others = sum(piece.shape[1] for piece in pieces)
    arrays = list(pieces) + list(carry or ())
    matrices = [project, keyval]
    if last:
        arrays.append(ending[0])
        matrices += ending[1:]
    rows = pieces[0].shape[1] if first else carry[0].shape[1]
    shapes = [jax.ShapeDtypeStruct((images, others, 2 * width), jnp.bfloat16)]
    if first:
        shapes.append(jax.ShapeDtypeStruct((images, rows, width), jnp.bfloat16))
    if last:
        shapes.append(jax.ShapeDtypeStruct((images, rows, model), jnp.float32))
        shapes.append(jax.ShapeDtypeStruct((images, rows, width), jnp.bfloat16))
    else:
        shapes.append(jax.ShapeDtypeStruct((images, HEADS, rows, LANES), jnp.float32))
    return pl.pallas_call(
        functools.partial(self_kernel, first, last, len(pieces)),
        grid=(images,),
        out_shape=shapes,
        in_specs=[per_image(array.shape) for array in arrays] + [whole(matrix) for matrix in matrices],
        out_specs=[per_image(shape.shape) for shape in shapes],
        scratch_shapes=[pltpu.VMEM((others, 2 * width), jnp.bfloat16)],
        compiler_params=pltpu.CompilerParams(vmem_limit_bytes=VMEM_BYTES),
        cost_estimate=pl.CostEstimate(
            flops=2 * images * (others * model * 4 * width + 4 * rows * others * width),
            bytes_accessed=2 * sum(matrix.size for matrix in matrices)
            + sum(array.size * array.dtype.itemsize for array in arrays),
            transcendentals=images * HEADS * rows * others,
        ),
        name="self_step",
    )(*arrays, *matrices)


def cross_kernel(pieces, after_ref, query_ref, *refs):
    keyval_refs, output_ref, out_ref = refs[:pieces], refs[pieces], refs[pieces + 1]
    width = output_ref.shape[0]
    halves, blocks, block_rows, part = out_ref.shape[1:]
    queries = query_ref[0]
    totals = nothing(queries.shape[0])
    for ref in keyval_refs:
        keyval = ref.at[0]
        totals = fold(queries, keyval, keyval, 0, width, totals)
    mixed = after_ref[0] + f32_dot(finish(totals), output_ref[...])
    for half in range(halves):
        columns = mixed[:, half * part : (half + 1) * part]
        out_ref[0, half] = columns.reshape(blocks, block_rows, part).astype(jnp.bfloat16)


def cross_block(after, query, keyvals, output, halves, block_rows):
    images, rows, model = after.shape
    width = output.shape[0]
    everyone = sum(keyval.shape[1] for keyval in keyvals)
    shape = (images, halves, rows // block_rows, block_rows, model // halves)
    return pl.pallas_call(
        functools.partial(cross_kernel, len(keyvals)),
        grid=(images,),
        out_shape=jax.ShapeDtypeStruct(shape, jnp.bfloat16),
        in_specs=[per_image(after.shape), per_image(query.shape)]
        + [
            pl.BlockSpec((1,) + keyval.shape[1:], lambda i: (images - 1 - i, 0, 0))
            for keyval in keyvals
        ]
        + [whole(output)],
        out_specs=per_image(shape),
        compiler_params=pltpu.CompilerParams(vmem_limit_bytes=VMEM_BYTES),
        cost_estimate=pl.CostEstimate(
            flops=2 * images * (4 * rows * everyone * width + rows * model * width),
            bytes_accessed=4 * after.size + 2 * (query.size + output.size + after.size),
            transcendentals=images * HEADS * rows * everyone,
        ),
        name="cross_block",
    )(after, query, *keyvals, output)


def shards(tokens, pair_list, owner_base, *weight_shards):
    groups = lax.axis_size("x")
    row_devices = lax.axis_size("z") * lax.axis_size("c")
    devices = groups * row_devices
    column = lax.axis_index("z") * lax.axis_size("c") + lax.axis_index("c")
    spread, block_rows, encoder = tokens.shape[1], tokens.shape[3], tokens.shape[4]
    held = tokens.reshape(spread, block_rows, encoder)
    part = encoder // groups

    x = lax.axis_index("x")
    parted = jnp.stack([held[:, :, i * part : (i + 1) * part] for i in range(groups)])
    parted, weight_shards = lax.optimization_barrier((parted, weight_shards))
    along_z = start_weights(weight_shards)
    pieces = []
    for step in range(groups):
        piece = lax.dynamic_index_in_dim(parted, (x + step) % groups, axis=0, keepdims=False)
        pieces.append(piece if step == 0 else pass_on(piece, "x", step))
    pieces = jnp.concatenate(pieces, axis=0)

    bases = owner_base[pair_list]
    slot = (column - bases) % spread
    source = ((bases + slot - column) // row_devices) % groups
    place = source * spread + slot
    held_at = (x - source) % groups * spread + slot
    outgoing = jnp.take(pieces, held_at.reshape(-1), axis=0, mode="clip").reshape(
        devices, 2, block_rows, part
    )
    outgoing, along_z = lax.optimization_barrier((outgoing, along_z))
    arrived = lax.all_to_all(outgoing, IMG, 0, 0, tiled=True)
    arrived = arrived.reshape(groups, row_devices, 2, block_rows, part)
    embed_full, rest = spread_weights(*order_weights(along_z))
    model_width = embed_full.shape[1]
    rest_left, rest_right = near_on_ring(rest, "tok")
    embedded = embed(arrived, embed_full)
    rest_left, rest_right, embedded = lax.optimization_barrier((rest_left, rest_right, embedded))
    near = near_on_ring(embedded, "tok")
    full, (left, right) = finish_weights(rest, rest_left, rest_right, near)
    project_full, self_out_full, query_full, keyval_full, cross_out_full = full
    far_low, far_high = ring_far(left, right, 1)
    near_keyval, queries, totals = self_step([left, right, embedded], project_full, keyval_full)
    far_keyval, after_self, cross_queries = self_step(
        [far_low, far_high], project_full, keyval_full, (queries, totals),
        (embedded, self_out_full, query_full),
    )

    halves = groups // 2
    backward = cross_block(
        after_self, cross_queries, [near_keyval, far_keyval], cross_out_full,
        halves, block_rows,
    ).reshape(devices, block_rows, model_width // halves)
    returned = lax.all_to_all(backward, IMG, 0, 0, tiled=True)
    my_half = x // halves
    my_place = lax.dynamic_index_in_dim(place, my_half, axis=1, keepdims=False)
    selector = (
        my_place[None, :] == jnp.arange(devices, dtype=jnp.int32)[:, None]
    ).astype(jnp.bfloat16)
    partial = jnp.einsum(
        "ge,ebd->gbd", selector, returned, preferred_element_type=jnp.float32
    ).astype(jnp.bfloat16)
    home = lax.all_to_all(
        partial.reshape(groups, spread, block_rows, model_width // halves), "x", 0, 0, tiled=True
    )
    home = home.reshape(2, halves, spread, block_rows, model_width // halves)
    total = home[0].astype(jnp.float32) + home[1].astype(jnp.float32)
    summed = jnp.concatenate([total[half] for half in range(halves)], axis=-1)
    return summed.astype(jnp.bfloat16).reshape(1, spread, 1, block_rows, model_width)


def solution(mesh):
    chips = Mesh(mesh.devices.reshape(4, 16, 2, 4), ("x", "z", "c", "tok"))
    rows = P(IMG, None)
    tokens = P(IMG, None, "tok", None, None)
    return jax.shard_map(
        shards,
        mesh=chips,
        in_specs=(tokens, P(), P()) + (rows,) * 6,
        out_specs=tokens,
        check_vma=False,
    )
```
